32 devices in a mesh: seq: 16 (over z, y, core), head: 2 (over x).
Axes of the slice: x: 2, y: 2, z: 4, core: 2. Of those that a mesh axis runs over, the one named last changes fastest.
Arguments:
- tokens: bfloat16 [8192, 1024], P('seq'), may hold values from -40 to 40
- w_qkv: bfloat16 [1024, 3072], P(None, 'head'), may hold values from -1 to 1
- w_out: bfloat16 [1024, 1024], P('head'), may hold values from -0.1875 to 0.1875
- offsets: int32 [5, 8], replicated, may hold values from 0 to 15, as said below
Outputs:
- mixed: bfloat16 [8192, 1024], P(('seq', 'head'))
The draws below stay inside these ranges and needn't reach their ends.
Inputs may be any that keep to these rules, and one draw needn't show every extreme that they name: offsets[b, h] lies in 0 .. 2^b - 1.
All inputs are finite; a program needn't handle non-finite values.
Results may differ from the reference program's by a relative error of at most 0.019.
Values may be sent and summed in bfloat16 or wider, within the bound.
No kernel may reach another device: no remote copies, remote signals or barrier semaphores. Data moves between devices by JAX's collectives and lax.ppermute only.
A program may use at most 128 MiB of HBM per device.

```python
import math
import jax
import jax.numpy as jnp
from jax import lax

D = 1024
H = 8
HD = 128
NB = 5
TOKENS = 8192
SEG = 512


def draw_tokens(key, part):
    base = jax.random.truncated_normal(key, -6.0, 6.0, (TOKENS, D), jnp.float32)
    return base.astype(jnp.bfloat16)


def draw_w_qkv(key, part):
    base = jax.random.truncated_normal(key, -6.0, 6.0, (D, H, 3, HD), jnp.float32) / math.sqrt(D)
    return base.reshape(D, 3 * D).astype(jnp.bfloat16)


def draw_offsets(key, part):
    limits = 2 ** jnp.arange(NB, dtype=jnp.int32)
    raw = jax.random.randint(key, (NB, H), 0, 2 ** (NB - 1), dtype=jnp.int32)
    chosen = jax.random.randint(jax.random.fold_in(key, 31), (), 0, H, dtype=jnp.int32)
    column = jnp.arange(H, dtype=jnp.int32)[None, :] == chosen
    return jnp.where(column, limits[:, None] - 1, raw % limits[:, None])


def block_scale(key, shape, cuts, least, top_value):
    loudness = 1.0
    for position, shards_of in cuts:
        steps = jax.random.uniform(jax.random.fold_in(jax.random.fold_in(key, 6), position), (shards_of,), jnp.float32, least / len(cuts), top_value / len(cuts))
        loudness = loudness * jnp.repeat(jnp.exp(steps), shape[position] // shards_of).reshape((-1,) + (1,) * (len(shape) - 1 - position))
    return loudness


def normal_values(key, extent, width, limit, shards=(), held_as=jnp.bfloat16):
    values = jax.random.normal(key, extent, jnp.float32) * width
    if len(shards) > 0:
        values = block_scale(key, extent, shards, -0.22, 0.18) * values
    return jnp.clip(values, min=-limit, max=limit).astype(held_as)


def setup_inputs(seed: int = 0) -> dict:
    arg_keys = jax.random.split(jax.random.key(seed), 5)
    tokens = draw_tokens(jax.random.fold_in(arg_keys[4], 71), 0)
    w_qkv = draw_w_qkv(jax.random.fold_in(arg_keys[4], 71), 0)
    w_out = normal_values(arg_keys[2], (D, D), D ** -0.5, 0.1875, ((0, 2),))
    offsets = draw_offsets(jax.random.fold_in(arg_keys[4], 71), 0)
    return {"tokens": tokens, "w_qkv": w_qkv, "w_out": w_out, "offsets": offsets}


def pick_rows(source_block, offset, stride):
    shaped = source_block.reshape(source_block.shape[0] // stride, stride, source_block.shape[1])
    return lax.dynamic_index_in_dim(shaped, offset, 1, keepdims=False)

def restore(values, offset, stride):
    value_rows = values.shape[0]
    expanded = values[:, None]
    onehot = (jnp.arange(stride, dtype=jnp.int32) == offset).reshape((1, stride) + (1,) * (values.ndim - 1))
    filled = jnp.where(onehot, expanded, jnp.zeros_like(expanded))
    return filled.reshape((value_rows * stride,) + values.shape[1:])

def attend(query, key_values, score_scale):
    head_dim = query.shape[1]
    query32 = query.astype(jnp.float32)
    keys32 = key_values[:, :head_dim].astype(jnp.float32)
    scores = jnp.dot(query32, keys32.T, preferred_element_type=jnp.float32) * score_scale
    row_max = lax.optimization_barrier(jnp.max(scores, axis=1))
    expo = jnp.exp(scores - row_max[:, None])
    row_sum = lax.optimization_barrier(jnp.sum(expo, axis=1))
    weighted = jnp.dot(expo.astype(jnp.bfloat16), key_values[:, head_dim:], preferred_element_type=jnp.float32)
    return (row_max, row_sum, weighted)

def merge_branch(running, row_max, row_sum, weighted, offset, stride):
    max_full = restore(row_max, offset, stride)
    sum_full = restore(row_sum, offset, stride)
    weighted_full = restore(weighted, offset, stride)
    if running is None:
        return (max_full, sum_full, weighted_full)
    run_max, run_sum, summed = running
    selected = jnp.arange(run_max.shape[0], dtype=jnp.int32) % stride == offset
    branch_max = jnp.where(selected, max_full, run_max)
    new_max = jnp.maximum(run_max, branch_max)
    decay_old = jnp.exp(run_max - new_max)
    weight_new = jnp.where(selected, jnp.exp(branch_max - new_max), jnp.zeros_like(new_max))
    run_sum = run_sum * decay_old + weight_new * sum_full
    summed = summed * decay_old[:, None] + weight_new[:, None] * weighted_full
    return (new_max, run_sum, summed)

def reference(tokens, w_qkv, w_out, offsets):
    score_scale = 1.0 / math.sqrt(HD)
    outputs = []
    for head_index in range(H):
        base_col = head_index * 3 * HD
        projected = jnp.dot(tokens, w_qkv[:, base_col:base_col + 3 * HD], preferred_element_type=jnp.float32).astype(jnp.bfloat16)
        queries = projected[:, :HD]
        key_values = projected[:, HD:]
        running = None
        for branch in range(NB):
            stride = 2 ** branch
            offset = offsets[branch, head_index]
            chosen_q = pick_rows(queries, offset, stride)
            chosen_kv = pick_rows(key_values, offset, stride)
            groups = chosen_q.shape[0] // SEG

            def per_segment(operand):
                return attend(operand[0], operand[1], score_scale)
            row_max, row_sum, weighted = lax.map(per_segment, (chosen_q.reshape(groups, SEG, HD), chosen_kv.reshape(groups, SEG, 2 * HD)))
            running = merge_branch(running, row_max.reshape(-1), row_sum.reshape(-1), weighted.reshape(-1, HD), offset, stride)
        run_max, run_sum, summed = running
        outputs.append((summed / run_sum[:, None]).astype(jnp.bfloat16))
    attended = jnp.concatenate(outputs, axis=1)
    return jnp.dot(attended, w_out, preferred_element_type=jnp.float32).astype(jnp.bfloat16)
```

```python
import functools
import math

import jax
import jax.numpy as jnp
from jax import lax
from jax.experimental import pallas as pl
from jax.experimental.pallas import tpu as pltpu
from jax.sharding import PartitionSpec as P

HD = 128
NB = 5
LATE = (2, 3, 4)
BF16 = jnp.bfloat16
F32 = jnp.float32
UNIT = math.log2(math.e) / math.sqrt(HD)
VMEM_LIMIT = 48 << 20
ANY = pl.BlockSpec(memory_space=pl.ANY)
SMEM = pl.BlockSpec(memory_space=pltpu.SMEM)
VMEM = pl.BlockSpec(memory_space=pltpu.VMEM)


def shape(*extent, dtype=BF16):
    return jax.ShapeDtypeStruct(extent, dtype)


class Copies:
    def __init__(self, sems):
        self.sems = sems
        self.used = 0

    def start(self, source, target):
        copy = pltpu.make_async_copy(source, target, self.sems.at[self.used])
        self.used += 1
        copy.start()
        return copy


def wait_all(copies):
    for copy in copies:
        copy.wait()


def project_kernel(halves, offs, tok_hbm, w_hbm, wo_hbm, *refs):
    heads = w_hbm.shape[1] // (3 * HD)
    rows = tok_hbm.shape[0]
    outs, (tok, w, kv, picks, wide, sems) = refs[:-6], refs[-6:]
    first = lax.axis_index("head") * heads
    copies = Copies(sems)
    loads = [copies.start(w_hbm.at[:, pl.ds(HD, 2 * HD)], w.at[0]), copies.start(tok_hbm, tok)]
    for head in range(1, heads):
        columns = pl.ds(head * 3 * HD + HD, 2 * HD)
        loads.append(copies.start(w_hbm.at[:, columns], w.at[head]))
    stores = []
    if halves:
        depth = wo_hbm.shape[0] // 2
        part = lax.rem(lax.axis_index("seq"), 2)
        source = wo_hbm.at[pl.ds(pl.multiple_of(part * depth, depth), depth)]
        stores.append(copies.start(source, outs[NB]))
    loads[1].wait()
    for head in range(heads):
        loads[0 if head == 0 else head + 1].wait()
        both = jnp.dot(tok[...], w[head], preferred_element_type=F32).astype(BF16)
        kv[head] = both
        stores.append(copies.start(kv.at[head], outs[0].at[head]))
        both = both.astype(F32)
        for c in range(2):
            wide[2 * head + c] = both[:, c * HD : (c + 1) * HD]
        low = 0
        for b in range(1, NB):
            n = rows >> b
            offset = offs[b, first + head]
            for c in range(2):
                picked = wide[2 * head + c, pl.ds(offset, n, stride=1 << b), :]
                picks[head, low : low + n, c * HD : (c + 1) * HD] = picked.astype(BF16)
            stores.append(
                copies.start(picks.at[head, pl.ds(low, n)], outs[b].at[head])
            )
            low += n
    wait_all(stores)


def project(offsets, tokens, w_qkv, w_out, halves):
    heads = w_qkv.shape[1] // (3 * HD)
    rows, width = tokens.shape
    out_shape = [shape(heads, rows >> b, 2 * HD) for b in range(NB)]
    if halves:
        out_shape.append(shape(w_out.shape[0] // 2, w_out.shape[1]))
    return pl.pallas_call(
        functools.partial(project_kernel, halves),
        in_specs=[SMEM, ANY, ANY, ANY],
        out_specs=[ANY] * len(out_shape),
        out_shape=out_shape,
        scratch_shapes=[
            pltpu.VMEM((rows, width), BF16),
            pltpu.VMEM((heads, width, 2 * HD), BF16),
            pltpu.VMEM((heads, rows, 2 * HD), BF16),
            pltpu.VMEM((heads, rows, 2 * HD), BF16),
            pltpu.VMEM((2 * heads, rows, HD), F32),
            pltpu.SemaphoreType.DMA((2 + 6 * heads,)),
        ],
        compiler_params=pltpu.CompilerParams(vmem_limit_bytes=VMEM_LIMIT),
        name="project",
    )(offsets, tokens, w_qkv, w_out)


def load_pieces(copies, pieces, target):
    low, started = 0, []
    for piece in pieces:
        n = piece.shape[1]
        started.append(copies.start(piece, target.at[:, pl.ds(low, n)]))
        low += n
    return started


def attend(query, keys, values):
    scores = lax.dot_general(
        query, keys, (((1,), (1,)), ((), ())), preferred_element_type=F32
    )
    top = jnp.max(scores, axis=1, keepdims=True)
    probs = jnp.exp2((scores - top) * UNIT).astype(BF16)
    both = jnp.dot(probs, values, preferred_element_type=F32)
    top = jnp.broadcast_to(top * UNIT, (query.shape[0], HD))
    return top, both[:, HD:], both[:, :HD]


def merge(state, head, picked, found):
    top_ref, sum_ref, value_ref = state
    top, row_sum, value = found
    old = top_ref[head, picked, :]
    new = jnp.maximum(old, top)
    decay, weight = jnp.exp2(old - new), jnp.exp2(top - new)
    top_ref[head, picked, :] = new
    sum_ref[head, picked, :] = sum_ref[head, picked, :] * decay + row_sum * weight
    value_ref[head, picked, :] = value_ref[head, picked, :] * decay + value * weight


def early_kernel(counts, parts, offs, tok_hbm, w_hbm, *refs):
    first_count, second_count = counts
    pieces = [refs[:first_count], refs[first_count : first_count + second_count]]
    refs = refs[first_count + second_count :]
    outs, late_query, late_value, late_stats = refs[:parts], *refs[parts : parts + 3]
    tok, w, kv0, kv1, values, query, top, row_sum, value, sems = refs[parts + 3 :]
    heads = w_hbm.shape[1] // (3 * HD)
    rows = tok.shape[0]
    part_rows = rows // parts
    me = lax.axis_index("head")
    copies = Copies(sems)
    loads = [copies.start(tok_hbm, tok)]
    for head in range(heads):
        columns = pl.ds(head * 3 * HD, HD)
        loads.append(copies.start(w_hbm.at[:, columns], w.at[:, pl.ds(head * HD, HD)]))
    kv_loads = [load_pieces(copies, pieces[b], (kv0, kv1)[b]) for b in range(2)]
    values[:, HD:] = jnp.ones((values.shape[0], HD), BF16)
    wait_all(loads)
    projected = jnp.dot(tok[...], w[...], preferred_element_type=F32).astype(BF16).astype(F32)
    for head in range(heads):
        query[head] = projected[:, head * HD : (head + 1) * HD]
    wait_all(kv_loads[0])
    state = (top, row_sum, value)
    step = min(rows, 256)
    for head in range(heads):
        values[:, :HD] = kv0[head, :, HD:]
        for low in range(0, rows, step):
            span = pl.ds(low, step)
            found = attend(query[head, span, :].astype(BF16), kv0[head, :, :HD], values[...])
            for ref, array in zip(state, found):
                ref[head, span, :] = array
    wait_all(kv_loads[1])
    for head in range(heads):
        values[:, :HD] = kv1[head, :, HD:]
        picked = pl.ds(offs[1, me * heads + head], rows // 2, stride=2)
        found = attend(query[head, picked, :].astype(BF16), kv1[head, :, :HD], values[...])
        merge(state, head, picked, found)
    for head in range(heads):
        columns = slice(head * HD, (head + 1) * HD)
        for d in range(parts):
            span = pl.ds(pl.multiple_of((me ^ d) * part_rows, part_rows), part_rows)
            outs[d][:, columns] = (value[head, span, :] / row_sum[head, span, :]).astype(BF16)
        low = 0
        for b in LATE:
            n = rows >> b
            picked = pl.ds(offs[b, me * heads + head], n, stride=1 << b)
            late_query[head, low : low + n, :] = query[head, picked, :].astype(BF16)
            late_value[head, low : low + n, :] = value[head, picked, :]
            late_stats[head, low : low + n, : HD // 2] = top[head, picked, :][:, : HD // 2]
            late_stats[head, low : low + n, HD // 2 :] = row_sum[head, picked, :][:, HD // 2 :]
            low += n


def early(offsets, tokens, w_qkv, pieces, parts):
    heads = w_qkv.shape[1] // (3 * HD)
    rows, width = tokens.shape
    keys = sum(piece.shape[1] for piece in pieces[0])
    late = sum(rows >> b for b in LATE)
    counts = [len(p) for p in pieces]
    out_shape = [shape(rows // parts, heads * HD)] * parts + [
        shape(heads, late, HD),
        shape(heads, late, HD, dtype=F32),
        shape(heads, late, HD, dtype=F32),
    ]
    return pl.pallas_call(
        functools.partial(early_kernel, counts, parts),
        in_specs=[SMEM] + [ANY] * (2 + sum(counts)),
        out_specs=[VMEM] * len(out_shape),
        out_shape=out_shape,
        scratch_shapes=[
            pltpu.VMEM((rows, width), BF16),
            pltpu.VMEM((width, heads * HD), BF16),
            pltpu.VMEM((heads, keys, 2 * HD), BF16),
            pltpu.VMEM((heads, keys, 2 * HD), BF16),
            pltpu.VMEM((keys, 2 * HD), BF16),
            pltpu.VMEM((heads, rows, HD), F32),
            pltpu.VMEM((heads, rows, HD), F32),
            pltpu.VMEM((heads, rows, HD), F32),
            pltpu.VMEM((heads, rows, HD), F32),
            pltpu.SemaphoreType.DMA((1 + heads + sum(counts),)),
        ],
        compiler_params=pltpu.CompilerParams(vmem_limit_bytes=VMEM_LIMIT),
        name="early",
    )(offsets, tokens, w_qkv, *pieces[0], *pieces[1])


def late_kernel(counts, parts, offs, late_query, late_value, late_stats, *refs):
    pieces = []
    for count in counts:
        pieces.append(refs[:count])
        refs = refs[count:]
    outs, (kv, values, top, row_sum, value, chosen, sems) = refs[:parts], refs[parts:]
    heads = late_query.shape[0]
    rows = top.shape[1]
    me = lax.axis_index("head")
    copies = Copies(sems)
    loads = [load_pieces(copies, pieces[i], kv.at[i]) for i in range(len(LATE))]
    values[:, HD:] = jnp.ones((values.shape[0], HD), BF16)
    state = (top, row_sum, value)
    for head in range(heads):
        low = 0
        for b in LATE:
            n = rows >> b
            picked = pl.ds(offs[b, me * heads + head], n, stride=1 << b)
            stats = late_stats[head, low : low + n, :]
            top[head, picked, :] = jnp.broadcast_to(stats[:, :1], (n, HD))
            row_sum[head, picked, :] = jnp.broadcast_to(stats[:, HD // 2 : HD // 2 + 1], (n, HD))
            value[head, picked, :] = late_value[head, low : low + n, :]
            low += n
    low = 0
    for i, b in enumerate(LATE):
        n = rows >> b
        wait_all(loads[i])
        for head in range(heads):
            values[:, :HD] = kv[i, head, :, HD:]
            picked = pl.ds(offs[b, me * heads + head], n, stride=1 << b)
            found = attend(late_query[head, low : low + n, :], kv[i, head, :, :HD], values[...])
            merge(state, head, picked, found)
        low += n
    for head in range(heads):
        for d in range(parts):
            low = 0
            for b in LATE:
                n = (rows >> b) // parts
                base = (me ^ d) * (rows // parts) + offs[b, me * heads + head]
                picked = pl.ds(base, n, stride=1 << b)
                chosen[low : low + n, :] = value[head, picked, :] / row_sum[head, picked, :]
                low += n
            outs[d][head] = chosen[...].astype(BF16)


def late(offsets, rows, late_query, late_value, late_stats, pieces, parts):
    heads = late_query.shape[0]
    keys = sum(piece.shape[1] for piece in pieces[0])
    counts = [len(p) for p in pieces]
    compact = sum((rows >> b) // parts for b in LATE)
    return pl.pallas_call(
        functools.partial(late_kernel, counts, parts),
        in_specs=[SMEM, VMEM, VMEM, VMEM] + [ANY] * sum(counts),
        out_specs=[VMEM] * parts,
        out_shape=[shape(heads, compact, HD)] * parts,
        scratch_shapes=[
            pltpu.VMEM((len(LATE), heads, keys, 2 * HD), BF16),
            pltpu.VMEM((keys, 2 * HD), BF16),
            pltpu.VMEM((heads, rows, HD), F32),
            pltpu.VMEM((heads, rows, HD), F32),
            pltpu.VMEM((heads, rows, HD), F32),
            pltpu.VMEM((compact, HD), F32),
            pltpu.SemaphoreType.DMA((sum(counts),)),
        ],
        compiler_params=pltpu.CompilerParams(vmem_limit_bytes=VMEM_LIMIT),
        name="late",
    )(offsets, late_query, late_value, late_stats, *pieces[0], *pieces[1], *pieces[2])


def mix_kernel(parts, heads, halves, offs, *refs):
    early_refs, late_refs = refs[:parts], refs[parts : 2 * parts]
    refs = refs[2 * parts :]
    w_refs = refs[: parts + halves]
    out, wide, narrow, joined = refs[parts + halves :]
    rows = out.shape[0]
    me = lax.axis_index("head")
    total = None
    for d in range(parts):
        for head in range(heads):
            wide[...] = early_refs[d][:, head * HD : (head + 1) * HD].astype(F32)
            narrow[...] = late_refs[d][head].astype(F32)
            low = 0
            for b in LATE:
                n = rows >> b
                picked = pl.ds(offs[b, (me ^ d) * heads + head], n, stride=1 << b)
                wide[picked, :] = narrow[low : low + n, :]
                low += n
            joined[:, head * HD : (head + 1) * HD] = wide[...].astype(BF16)
        if halves and d == 1:
            part = lax.rem(lax.axis_index("seq"), 2)
            depth = w_refs[1].shape[0]
            for i in range(2):
                columns = pl.ds(pl.multiple_of((part ^ i) * depth, depth), depth)
                total += jnp.dot(joined[:, columns], w_refs[1 + i][...], preferred_element_type=F32)
        else:
            term = jnp.dot(joined[...], w_refs[d][...], preferred_element_type=F32)
            total = term if total is None else total + term
    out[...] = total.astype(BF16)


def mix(offsets, early_parts, late_parts, weights, halves):
    parts = len(early_parts)
    heads, compact, _ = late_parts[0].shape
    rows, columns = early_parts[0].shape
    width = weights[0].shape[1]
    return pl.pallas_call(
        functools.partial(mix_kernel, parts, heads, halves),
        in_specs=[SMEM] + [VMEM] * (2 * parts + len(weights)),
        out_specs=VMEM,
        out_shape=shape(rows, width),
        scratch_shapes=[
            pltpu.VMEM((rows, HD), F32),
            pltpu.VMEM((compact, HD), F32),
            pltpu.VMEM((rows, columns), BF16),
        ],
        compiler_params=pltpu.CompilerParams(vmem_limit_bytes=VMEM_LIMIT),
        name="mix",
    )(offsets, *early_parts, *late_parts, *weights)


def swap(x, axis, distance):
    return lax.ppermute(x, axis, [(i, i ^ distance) for i in range(lax.axis_size(axis))])


def spread(pieces, distances):
    for distance in distances:
        pieces = pieces + [swap(piece, "seq", distance) for piece in pieces]
    return pieces


def on_device(tokens, w_qkv, w_out, offsets):
    seq, parts = lax.axis_size("seq"), lax.axis_size("head")
    rows = tokens.shape[0]
    halves = seq == 16 and parts == 2
    own = project(offsets, tokens, w_qkv, w_out, halves)
    if halves:
        y3 = swap(own[3], "seq", 2)
        y2 = swap(own[2], "seq", 2)
        z4 = [own[4]] + [swap(own[4], "seq", d) for d in (12, 8, 4)]
        z3 = swap(own[3], "seq", 4)
        w_half = swap(own[NB], "head", 1)
        gathered = [
            [own[0]],
            spread([own[1]], [1]),
            spread([own[2], y2], [1]),
            spread([own[3], y3, z3, swap(y3, "seq", 4)], [1]),
            spread(z4, [2, 1]),
        ]
        weights = [w_out, w_half, swap(w_half, "seq", 1)]
    else:
        gathered = []
        for b in range(NB):
            steps = (seq * (1 << b) // 16).bit_length() - 1
            pieces = own[b]
            for step in range(steps):
                pieces = jnp.concatenate([pieces, swap(pieces, "seq", 1 << step)], axis=1)
            gathered.append([pieces])
        weights = [w_out] + [swap(w_out, "head", d) for d in range(1, parts)]
    *early_parts, late_query, late_value, late_stats = early(
        offsets, tokens, w_qkv, gathered[:2], parts
    )
    early_parts = [early_parts[0]] + [
        swap(early_parts[d], "head", d) for d in range(1, parts)
    ]
    late_parts = late(offsets, rows, late_query, late_value, late_stats, gathered[2:], parts)
    late_parts = [late_parts[0]] + [swap(late_parts[d], "head", d) for d in range(1, parts)]
    return mix(offsets, early_parts, late_parts, weights, int(halves))


def solution(mesh):
    in_specs = (P("seq", None), P(None, "head"), P("head", None), P())
    out_specs = P(("seq", "head"), None)
    return jax.shard_map(
        on_device, mesh=mesh, in_specs=in_specs, out_specs=out_specs, check_vma=False
    )
```

```python
import functools
import math

import jax
import jax.numpy as jnp
from jax import lax
from jax.experimental import pallas as pl
from jax.experimental.pallas import tpu as pltpu
from jax.sharding import PartitionSpec as P

HD = 128
NB = 5
MIDDLE, LATE = (2,), (3, 4)
LATER = MIDDLE + LATE
BF16 = jnp.bfloat16
F32 = jnp.float32
UNIT = math.log2(math.e) / math.sqrt(HD)
VMEM_LIMIT = 24 << 20
ANY = pl.BlockSpec(memory_space=pl.ANY)
VMEM = pl.BlockSpec(memory_space=pltpu.VMEM)
HBM = pl.BlockSpec(memory_space=pltpu.HBM)


def shape(*extent, dtype=BF16):
    return jax.ShapeDtypeStruct(extent, dtype)


class Copies:
    def __init__(self, sems):
        self.sems = sems
        self.used = 0

    def start(self, source, target):
        copy = pltpu.make_async_copy(source, target, self.sems.at[self.used])
        self.used += 1
        copy.start()
        return copy


def wait_all(copies):
    for copy in copies:
        copy.wait()


def in_hbm(x):
    return pltpu.with_memory_space_constraint(x, pltpu.HBM)


def cost(microseconds):
    return pl.CostEstimate(
        flops=int(microseconds * 1e9), bytes_accessed=0, transcendentals=0
    )


def project_kernel(groups, halves, offs_hbm, tok_hbm, w_hbm, wo_hbm, *refs):
    heads = w_hbm.shape[1] // (3 * HD)
    rows = tok_hbm.shape[0]
    outs, (offs, w, wide, sems) = refs[:-4], refs[-4:]
    tok, outs = outs[0], outs[1:]
    first = lax.axis_index("head") * heads
    copies = Copies(sems)
    loads = [copies.start(tok_hbm, tok)]
    for head in range(heads):
        columns = pl.ds(head * 3 * HD + HD, 2 * HD)
        loads.append(copies.start(w_hbm.at[:, columns], w.at[head]))
    offs_load = copies.start(offs_hbm, offs)
    stores = []
    if halves:
        depth = wo_hbm.shape[0] // 2
        part = lax.rem(lax.axis_index("seq"), 2)
        source = wo_hbm.at[pl.ds(pl.multiple_of(part * depth, depth), depth)]
        stores.append(copies.start(source, outs[-1]))
    loads[0].wait()
    for head in range(heads + 1):
        if head < heads:
            loads[head + 1].wait()
            both = jnp.dot(tok[...], w[head], preferred_element_type=F32).astype(BF16)
            outs[0][head] = both
            both = both.astype(F32)
            for c in range(2):
                wide[2 * head + c] = both[:, c * HD : (c + 1) * HD]
        if head == 0:
            offs_load.wait()
            continue
        done = head - 1
        for b in range(1, NB):
            n = rows >> b
            offset = offs[b, first + done]
            for c in range(2):
                picked = wide[2 * done + c, pl.ds(offset, n, stride=1 << b), :].astype(BF16)
                for out, group in zip(outs[1:], groups):
                    if b in group:
                        low = sum(rows >> other for other in group[: group.index(b)])
                        out[done, low : low + n, c * HD : (c + 1) * HD] = picked
    wait_all(stores)


def project(offsets, tokens, w_qkv, w_out, groups, halves):
    heads = w_qkv.shape[1] // (3 * HD)
    rows, width = tokens.shape
    out_shape = [shape(rows, width), shape(heads, rows, 2 * HD)]
    for group in groups:
        out_shape.append(shape(heads, sum(rows >> b for b in group), 2 * HD))
    out_specs = [VMEM] * len(out_shape)
    if halves:
        out_shape.append(shape(w_out.shape[0] // 2, w_out.shape[1]))
        out_specs.append(ANY)
    return pl.pallas_call(
        functools.partial(project_kernel, groups, halves),
        in_specs=[HBM, HBM, HBM, HBM],
        out_specs=out_specs,
        out_shape=out_shape,
        scratch_shapes=[
            pltpu.SMEM(offsets.shape, jnp.int32),
            pltpu.VMEM((heads, width, 2 * HD), BF16),
            pltpu.VMEM((2 * heads, rows, HD), F32),
            pltpu.SemaphoreType.DMA((3 + heads,)),
        ],
        compiler_params=pltpu.CompilerParams(vmem_limit_bytes=VMEM_LIMIT),
        cost_estimate=cost(5),
        name="project",
    )(in_hbm(offsets), in_hbm(tokens), in_hbm(w_qkv), in_hbm(w_out))


def keys_and_values(refs, spans, head):
    parts = [ref[head, low : low + n, :] for ref, (low, n) in zip(refs, spans)]
    both = jnp.concatenate(parts, axis=0) if len(parts) > 1 else parts[0]
    ones = jnp.ones((both.shape[0], HD), BF16)
    return both[:, :HD], jnp.concatenate([both[:, HD:], ones], axis=1)


def operands(pieces):
    arrays, places = [], []
    for branch in pieces:
        found = []
        for array, low, n in branch:
            known = [i for i, other in enumerate(arrays) if other is array]
            if not known:
                known = [len(arrays)]
                arrays.append(array)
            found.append((known[0], low, n))
        places.append(found)
    return arrays, places


def branch_of(refs, places, head):
    return keys_and_values([refs[i] for i, _, _ in places], [(low, n) for _, low, n in places], head)


def attend(query, keys, values):
    scores = lax.dot_general(
        query, keys, (((1,), (1,)), ((), ())), preferred_element_type=F32
    )
    top = jnp.max(scores, axis=1, keepdims=True)
    probs = jnp.exp2((scores - top) * UNIT).astype(BF16)
    both = jnp.dot(probs, values, preferred_element_type=F32)
    top = jnp.broadcast_to(top * UNIT, (query.shape[0], HD))
    return top, both[:, HD:], both[:, :HD]


def merge(state, head, picked, found):
    top_ref, sum_ref, value_ref = state
    top, row_sum, value = found
    old = top_ref[head, picked, :]
    new = jnp.maximum(old, top)
    decay, weight = jnp.exp2(old - new), jnp.exp2(top - new)
    top_ref[head, picked, :] = new
    sum_ref[head, picked, :] = sum_ref[head, picked, :] * decay + row_sum * weight
    value_ref[head, picked, :] = value_ref[head, picked, :] * decay + value * weight


def compact_rows(branches, rows):
    return sum(rows >> b for b in branches)


def compact(state, head, picks, outs):
    low = 0
    for picked in picks:
        for ref, out in zip(state, outs):
            out[head, low : low + picked.size, :] = ref[head, picked, :]
        low += picked.size


def pick(offs, b, head, rows):
    return pl.ds(offs[b, head], rows >> b, stride=1 << b)


def early_kernel(count, places, parts, offs_hbm, tok, w_hbm, *refs):
    arrays, refs = refs[:count], refs[count:]
    outs, later_query, later = refs[:parts], refs[parts], refs[parts + 1 : parts + 4]
    offs, w_query, query, *state, sems = refs[parts + 4 :]
    heads, rows = query.shape[:2]
    part_rows = rows // parts
    me = lax.axis_index("head")
    copies = Copies(sems)
    loads = []
    for head in range(heads):
        source = w_hbm.at[:, pl.ds(head * 3 * HD, HD)]
        loads.append(copies.start(source, w_query.at[:, pl.ds(head * HD, HD)]))
    offs_load = copies.start(offs_hbm, offs)
    wait_all(loads)
    projected = jnp.dot(tok[...], w_query[...], preferred_element_type=F32).astype(BF16)
    step = min(rows, 256)
    offs_load.wait()
    for head in range(heads):
        mine = projected[:, head * HD : (head + 1) * HD]
        query[head] = mine.astype(F32)
        keys, values = branch_of(arrays, places[0], head)
        for low in range(0, rows, step):
            span = slice(low, low + step)
            for ref, array in zip(state, attend(mine[span], keys, values)):
                ref[head, span] = array
        keys, values = branch_of(arrays, places[1], head)
        picked = pick(offs, 1, me * heads + head, rows)
        merge(state, head, picked, attend(query[head, picked, :].astype(BF16), keys, values))
        _, row_sum, value = state
        columns = slice(head * HD, (head + 1) * HD)
        for d in range(parts):
            span = pl.ds(pl.multiple_of((me ^ d) * part_rows, part_rows), part_rows)
            outs[d][:, columns] = (value[head, span, :] / row_sum[head, span, :]).astype(BF16)
        picks = [pick(offs, b, me * heads + head, rows) for b in LATER]
        low = 0
        for picked in picks:
            later_query[head, low : low + picked.size, :] = query[head, picked, :].astype(BF16)
            low += picked.size
        compact(state, head, picks, later)


def early(offsets, tokens, w_qkv, pieces, parts):
    heads = w_qkv.shape[1] // (3 * HD)
    rows, width = tokens.shape
    arrays, places = operands(pieces)
    later = compact_rows(LATER, rows)
    out_shape = [shape(rows // parts, heads * HD)] * parts
    out_shape.append(shape(heads, later, HD))
    out_shape += [shape(heads, later, HD, dtype=F32)] * 3
    return pl.pallas_call(
        functools.partial(early_kernel, len(arrays), places, parts),
        in_specs=[HBM, VMEM, HBM] + [VMEM] * len(arrays),
        out_specs=[VMEM] * len(out_shape),
        out_shape=out_shape,
        scratch_shapes=[
            pltpu.SMEM(offsets.shape, jnp.int32),
            pltpu.VMEM((width, heads * HD), BF16),
            pltpu.VMEM((heads, rows, HD), F32),
            pltpu.VMEM((heads, rows, HD), F32),
            pltpu.VMEM((heads, rows, HD), F32),
            pltpu.VMEM((heads, rows, HD), F32),
            pltpu.SemaphoreType.DMA((1 + heads,)),
        ],
        compiler_params=pltpu.CompilerParams(vmem_limit_bytes=VMEM_LIMIT),
        cost_estimate=cost(4),
        name="early",
    )(in_hbm(offsets), tokens, in_hbm(w_qkv), *arrays)


def middle_kernel(count, places, parts, blocks, offs_hbm, query, top_in, sum_in, value_in, *refs):
    arrays, refs = refs[:count], refs[count:]
    ins, outs, refs = refs[:parts], refs[parts : 2 * parts], refs[2 * parts :]
    if blocks > 1:
        outs, refs = [outs[0], list(outs[1:]) + [refs[0]]], refs[1:]
    late_query, *late = refs[:4]
    offs, *state, wide, sems = refs[4:]
    _, row_sum, value = state
    heads, rows = value.shape[:2]
    part_rows = rows // parts
    me = lax.axis_index("head")
    offs_load = Copies(sems).start(offs_hbm, offs)
    (branch,) = MIDDLE
    own = rows >> branch
    found = []
    for head in range(heads):
        keys, values = branch_of(arrays, places[0], head)
        found.append(attend(query[head, :own, :], keys, values))
    offs_load.wait()
    for head in range(heads):
        picks = [pick(offs, b, me * heads + head, rows) for b in LATER]
        low = 0
        for picked in picks:
            for ref, array in zip(state, (top_in, sum_in, value_in)):
                ref[head, picked, :] = array[head, low : low + picked.size, :]
            low += picked.size
        merge(state, head, picks[0], found[head])
        columns = slice(head * HD, (head + 1) * HD)
        for d in range(parts):
            offset = offs[branch, me * heads + head]
            source = pl.ds((me ^ d) * part_rows + offset, part_rows >> branch, stride=1 << branch)
            target = pl.ds(offset, part_rows >> branch, stride=1 << branch)
            wide[head] = ins[d][:, columns].astype(F32)
            wide[head, target, :] = value[head, source, :] / row_sum[head, source, :]
            out, target = outs[d], columns
            if blocks > 1 and d > 0:
                per = heads // blocks
                out = out[head // per]
                target = slice(head % per * HD, (head % per + 1) * HD)
            out[:, target] = wide[head].astype(BF16)
        late_query[head] = query[head, own:, :]
        compact(state, head, picks[1:], late)


def middle(offsets, rows, query, state, parts_in, pieces, blocks=1):
    heads = query.shape[0]
    parts = len(parts_in)
    arrays, places = operands(pieces)
    late = compact_rows(LATE, rows)
    part_rows, columns = parts_in[0].shape
    out_shape = [shape(part_rows, columns)]
    out_shape += [shape(part_rows, columns // blocks)] * (parts - 1) * blocks
    out_shape += [shape(heads, late, HD)]
    out_shape += [shape(heads, late, HD, dtype=F32)] * 3
    return pl.pallas_call(
        functools.partial(middle_kernel, len(arrays), places, parts, blocks),
        in_specs=[HBM] + [VMEM] * (4 + len(arrays) + parts),
        out_specs=[VMEM] * len(out_shape),
        out_shape=out_shape,
        scratch_shapes=[
            pltpu.SMEM(offsets.shape, jnp.int32),
            pltpu.VMEM((heads, rows, HD), F32),
            pltpu.VMEM((heads, rows, HD), F32),
            pltpu.VMEM((heads, rows, HD), F32),
            pltpu.VMEM((heads, rows // parts, HD), F32),
            pltpu.SemaphoreType.DMA((1,)),
        ],
        compiler_params=pltpu.CompilerParams(vmem_limit_bytes=VMEM_LIMIT),
        cost_estimate=cost(0.01),
        name="middle",
    )(in_hbm(offsets), query, *state, *arrays, *parts_in)


def joined_state(old, found):
    top = jnp.maximum(old[0], found[0])
    decay, weight = jnp.exp2(old[0] - top), jnp.exp2(found[0] - top)
    return top, *(a * decay + b * weight for a, b in zip(old[1:], found[1:]))


def late_kernel(count, places, parts, offs_hbm, query, *refs):
    state_in, arrays, refs = refs[:3], refs[3 : 3 + count], refs[3 + count :]
    outs, (offs, *state, ratio, chosen, sems) = refs[:parts], refs[parts:]
    heads, n3 = state[0].shape[:2]
    n4 = n3 // 2
    me = lax.axis_index("head")
    offs_load = Copies(sems).start(offs_hbm, offs)
    third, fourth = LATE
    found = []
    for head in range(heads):
        spans = (slice(0, n3), slice(n3, n3 + n4))
        for places_of, span in zip(places, spans):
            keys, values = branch_of(arrays, places_of, head)
            found.append(attend(query[head, span, :], keys, values))
    for head in range(heads):
        new = joined_state([ref[head, :n3, :] for ref in state_in], found[2 * head])
        for ref, array in zip(state, new):
            ref[head] = array
        ratio[head, :n3, :] = new[2] / new[1]
    offs_load.wait()
    for head in range(heads):
        offset = offs[fourth, me * heads + head]
        nested = (offset & ((1 << third) - 1)) == offs[third, me * heads + head]
        inner = pl.ds(offset >> third, n4, stride=2)
        old = [
            jnp.where(nested, ref[head, inner, :], given[head, n3:, :])
            for ref, given in zip(state, state_in)
        ]
        new = joined_state(old, found[2 * head + 1])
        ratio[head, n3:, :] = new[2] / new[1]
        for d in range(parts):
            low = 0
            for start, n in ((0, n3 // parts), (n3, n4 // parts)):
                chosen[low : low + n, :] = ratio[head, pl.ds(start + (me ^ d) * n, n), :]
                low += n
            outs[d][head] = chosen[...].astype(BF16)


def late(offsets, rows, query, state, pieces, parts):
    heads = query.shape[0]
    arrays, places = operands(pieces)
    chosen = compact_rows(LATE, rows // parts)
    n3 = rows >> LATE[0]
    return pl.pallas_call(
        functools.partial(late_kernel, len(arrays), places, parts),
        in_specs=[HBM] + [VMEM] * (4 + len(arrays)),
        out_specs=[VMEM] * parts,
        out_shape=[shape(heads, chosen, HD)] * parts,
        scratch_shapes=[
            pltpu.SMEM(offsets.shape, jnp.int32),
            pltpu.VMEM((heads, n3, HD), F32),
            pltpu.VMEM((heads, n3, HD), F32),
            pltpu.VMEM((heads, n3, HD), F32),
            pltpu.VMEM((heads, compact_rows(LATE, rows), HD), F32),
            pltpu.VMEM((chosen, HD), F32),
            pltpu.SemaphoreType.DMA((1,)),
        ],
        compiler_params=pltpu.CompilerParams(vmem_limit_bytes=VMEM_LIMIT),
        cost_estimate=cost(2),
        name="late",
    )(in_hbm(offsets), query, *state, *arrays)


def mix_kernel(distances, heads, blocks, split, offs_hbm, *refs):
    count = len(distances)
    early_refs, refs = refs[: count * blocks], refs[count * blocks :]
    later_refs, refs = refs[:count], refs[count:]
    total = None
    if refs[0].dtype == F32:
        total, refs = refs[0][...], refs[1:]
    w_refs, (out, offs, wide, narrow, joined, sems) = refs[:-6], refs[-6:]
    rows = out.shape[0]
    me = lax.axis_index("head")
    offs_load = Copies(sems).start(offs_hbm, offs)
    for i, d in enumerate(distances):
        for head in range(heads):
            per = heads // blocks
            columns = slice(head % per * HD, (head % per + 1) * HD)
            wide[head] = early_refs[i * blocks + head // per][:, columns].astype(F32)
            narrow[head] = later_refs[i][head].astype(F32)
        if i == 0:
            offs_load.wait()
        for head in range(heads):
            low = 0
            for b in LATE:
                picked = pick(offs, b, (me ^ d) * heads + head, rows)
                wide[head, picked, :] = narrow[head, low : low + picked.size, :]
                low += picked.size
            joined[:, head * HD : (head + 1) * HD] = wide[head].astype(BF16)
        if split:
            part = lax.rem(lax.axis_index("seq"), 2)
            depth = w_refs[0].shape[0]
            columns = [pl.ds(pl.multiple_of((part ^ c) * depth, depth), depth) for c in range(2)]
            terms = [(joined[:, columns[c]], w_refs[c][...]) for c in range(2)]
        else:
            terms = [(joined[...], w_refs[i][...])]
        for left, right in terms:
            term = jnp.dot(left, right, preferred_element_type=F32)
            total = term if total is None else total + term
    out[...] = total.astype(out.dtype)


def mix(offsets, distances, early_parts, later_parts, weights, total, last):
    heads = later_parts[0].shape[0]
    rows, width = early_parts[0].shape[0], weights[0].shape[1]
    blocks = len(early_parts) // len(distances)
    split = len(weights) > len(distances)
    totals = [] if total is None else [total]
    arrays = [*early_parts, *later_parts, *totals, *weights]
    return pl.pallas_call(
        functools.partial(mix_kernel, distances, heads, blocks, split),
        in_specs=[HBM] + [VMEM] * len(arrays),
        out_specs=VMEM,
        out_shape=shape(rows, width, dtype=BF16 if last else F32),
        scratch_shapes=[
            pltpu.SMEM(offsets.shape, jnp.int32),
            pltpu.VMEM((heads, rows, HD), F32),
            pltpu.VMEM((heads, compact_rows(LATE, rows), HD), F32),
            pltpu.VMEM((rows, heads * HD), BF16),
            pltpu.SemaphoreType.DMA((1,)),
        ],
        compiler_params=pltpu.CompilerParams(vmem_limit_bytes=VMEM_LIMIT),
        cost_estimate=cost(1),
        name="mix",
    )(in_hbm(offsets), *arrays)


def swap(x, axis, distance):
    return lax.ppermute(x, axis, [(i, i ^ distance) for i in range(lax.axis_size(axis))])


def together(arrays):
    return list(lax.optimization_barrier(tuple(arrays)))


def pair(piece):
    return [piece, swap(piece, "seq", 1)]


def layer_16(tokens, w_qkv, w_out, offsets):
    parts = lax.axis_size("head")
    rows = tokens.shape[0]
    n1, n2, n3, n4 = (rows >> b for b in range(1, NB))
    groups = [(1, 4, 3, 2), (4, 3, 2), (4, 3), (4,)]
    tokens, kv, near, all_own, far, b4, w_half = project(
        offsets, tokens, w_qkv, w_out, groups, True
    )
    near_core = swap(near, "seq", 1)
    b4_z8, b4_z12 = swap(b4, "seq", 8), swap(b4, "seq", 12)
    far_z4 = swap(far, "seq", 4)
    w_half = swap(w_half, "head", 1)
    all_y = swap(all_own, "seq", 2)
    nears = [near, near_core]
    pieces = [[(kv, 0, rows)], [(piece, 0, n1) for piece in nears]]
    first, other, query, *state = early(offsets, tokens, w_qkv, pieces, parts)
    all_y, far_z4, b4_z8, b4_z12, query = together([all_y, far_z4, b4_z8, b4_z12, query])
    b4_z = jnp.concatenate([b4_z8, b4_z12], axis=1)
    b4_yz = swap(b4_z, "seq", 2)
    far_yz4 = swap(all_y[:, : n4 + n3], "seq", 4)
    alls, far_z4s, b4_zs = pair(all_y), pair(far_z4), pair(b4_z)
    pieces = [
        [(piece, n1 + n4 + n3, n2) for piece in nears] + [(piece, n4 + n3, n2) for piece in alls]
    ]
    first, *other, query, top, row_sum, value = middle(
        offsets, rows, query, state, [first, other], pieces, 2
    )
    state = [top, row_sum, value]
    w_half, *other = together([w_half, *other])
    other[0] = swap(other[0], "head", 1)
    other[1] = swap(together([other[1], other[0]])[0], "head", 1)
    early_parts = [first, other]
    far_yz4, b4_yz, query = together([far_yz4, b4_yz, query])
    fars = alls + far_z4s + pair(far_yz4)
    b4_zs = b4_zs + pair(b4_yz)
    pieces = [
        [(piece, n1 + n4, n3) for piece in nears] + [(piece, n4, n3) for piece in fars],
        [(piece, n1, n4) for piece in nears]
        + [(piece, 0, n4) for piece in fars]
        + [(piece, 0, 2 * n4) for piece in b4_zs],
    ]
    late_parts = late(offsets, rows, query, state, pieces, parts)
    late_part = swap(late_parts[1], "head", 1)
    total = mix(offsets, [0], early_parts[:1], late_parts[:1], [w_out], None, False)
    weights = [w_half, swap(w_half, "seq", 1)]
    return mix(offsets, [1], early_parts[1], [late_part], weights, total, True)


def exchange(own, seq):
    gathered = []
    for b in range(NB):
        pieces = own[b]
        for step in range((seq * (1 << b) // 16).bit_length() - 1):
            pieces = jnp.concatenate([pieces, swap(pieces, "seq", 1 << step)], axis=1)
        gathered.append([(pieces, 0, pieces.shape[1])])
    return gathered


def on_device(tokens, w_qkv, w_out, offsets):
    seq, parts = lax.axis_size("seq"), lax.axis_size("head")
    rows = tokens.shape[0]
    if seq == 16 and parts == 2:
        return layer_16(tokens, w_qkv, w_out, offsets)
    groups = [(b,) for b in range(1, NB)]
    tokens, *own = project(offsets, tokens, w_qkv, w_out, groups, False)
    gathered = exchange(own, seq)
    weights = [w_out] + [swap(w_out, "head", d) for d in range(1, parts)]
    *early_parts, query, top, row_sum, value = early(
        offsets, tokens, w_qkv, gathered[:2], parts
    )
    state = [top, row_sum, value]
    *early_parts, query, top, row_sum, value = middle(
        offsets, rows, query, state, early_parts, gathered[2:3]
    )
    state = [top, row_sum, value]
    late_parts = list(late(offsets, rows, query, state, gathered[3:], parts))
    for found in (early_parts, late_parts):
        found[1:] = [swap(found[d], "head", d) for d in range(1, parts)]
    return mix(offsets, list(range(parts)), early_parts, late_parts, weights, None, True)


def solution(mesh):
    in_specs = (P("seq", None), P(None, "head"), P("head", None), P())
    out_specs = P(("seq", "head"), None)
    return jax.shard_map(
        on_device, mesh=mesh, in_specs=in_specs, out_specs=out_specs, check_vma=False
    )
```

```python
import functools
import math

import jax
import jax.numpy as jnp
from jax import lax
from jax.experimental import pallas as pl
from jax.experimental.pallas import tpu as pltpu
from jax.sharding import PartitionSpec as P

HD = 128
NB = 5
MIDDLE, LATE = (2,), (3, 4)
LATER = MIDDLE + LATE
BF16 = jnp.bfloat16
F32 = jnp.float32
UNIT = math.log2(math.e) / math.sqrt(HD)
VMEM_LIMIT = 24 << 20
ANY = pl.BlockSpec(memory_space=pl.ANY)
VMEM = pl.BlockSpec(memory_space=pltpu.VMEM)
HBM = pl.BlockSpec(memory_space=pltpu.HBM)


def shape(*extent, dtype=BF16):
    return jax.ShapeDtypeStruct(extent, dtype)


class Copies:
    def __init__(self, sems):
        self.sems = sems
        self.used = 0

    def start(self, source, target):
        copy = pltpu.make_async_copy(source, target, self.sems.at[self.used])
        self.used += 1
        copy.start()
        return copy


def wait_all(copies):
    for copy in copies:
        copy.wait()


def in_hbm(x):
    return pltpu.with_memory_space_constraint(x, pltpu.HBM)


def cost(microseconds):
    return pl.CostEstimate(
        flops=int(microseconds * 1e9), bytes_accessed=0, transcendentals=0
    )


def project_kernel(groups, halves, offs_hbm, tok_hbm, w_hbm, wo_hbm, *refs):
    heads = w_hbm.shape[1] // (3 * HD)
    rows = tok_hbm.shape[0]
    outs, (offs, w, wide, sems) = refs[:-4], refs[-4:]
    tok, outs = outs[0], outs[1:]
    first = lax.axis_index("head") * heads
    copies = Copies(sems)
    loads = [copies.start(tok_hbm, tok)]
    for head in range(heads):
        columns = pl.ds(head * 3 * HD + HD, 2 * HD)
        loads.append(copies.start(w_hbm.at[:, columns], w.at[head]))
    offs_load = copies.start(offs_hbm, offs)
    stores = []
    if halves:
        depth = wo_hbm.shape[0] // 2
        part = lax.rem(lax.axis_index("seq"), 2)
        source = wo_hbm.at[pl.ds(pl.multiple_of(part * depth, depth), depth)]
        stores.append(copies.start(source, outs[-1]))
    loads[0].wait()
    for head in range(heads + 1):
        if head < heads:
            loads[head + 1].wait()
            both = jnp.dot(tok[...], w[head], preferred_element_type=F32).astype(BF16)
            outs[0][head] = both
            both = both.astype(F32)
            for c in range(2):
                wide[2 * head + c] = both[:, c * HD : (c + 1) * HD]
        if head == 0:
            offs_load.wait()
            continue
        done = head - 1
        for b in range(1, NB):
            n = rows >> b
            offset = offs[b, first + done]
            for c in range(2):
                picked = wide[2 * done + c, pl.ds(offset, n, stride=1 << b), :].astype(BF16)
                for out, group in zip(outs[1:], groups):
                    if b in group:
                        low = sum(rows >> other for other in group[: group.index(b)])
                        out[done, low : low + n, c * HD : (c + 1) * HD] = picked
    wait_all(stores)


def project(offsets, tokens, w_qkv, w_out, groups, halves):
    heads = w_qkv.shape[1] // (3 * HD)
    rows, width = tokens.shape
    out_shape = [shape(rows, width), shape(heads, rows, 2 * HD)]
    for group in groups:
        out_shape.append(shape(heads, sum(rows >> b for b in group), 2 * HD))
    out_specs = [VMEM] * len(out_shape)
    if halves:
        out_shape.append(shape(w_out.shape[0] // 2, w_out.shape[1]))
        out_specs.append(ANY)
    return pl.pallas_call(
        functools.partial(project_kernel, groups, halves),
        in_specs=[HBM, HBM, HBM, HBM],
        out_specs=out_specs,
        out_shape=out_shape,
        scratch_shapes=[
            pltpu.SMEM(offsets.shape, jnp.int32),
            pltpu.VMEM((heads, width, 2 * HD), BF16),
            pltpu.VMEM((2 * heads, rows, HD), F32),
            pltpu.SemaphoreType.DMA((3 + heads,)),
        ],
        compiler_params=pltpu.CompilerParams(vmem_limit_bytes=VMEM_LIMIT),
        cost_estimate=cost(5),
        name="project",
    )(in_hbm(offsets), in_hbm(tokens), in_hbm(w_qkv), in_hbm(w_out))


def keys_and_values(refs, spans, head):
    parts = [ref[head, low : low + n, :] for ref, (low, n) in zip(refs, spans)]
    both = jnp.concatenate(parts, axis=0) if len(parts) > 1 else parts[0]
    ones = jnp.ones((both.shape[0], HD), BF16)
    return both[:, :HD], jnp.concatenate([both[:, HD:], ones], axis=1)


def operands(pieces):
    arrays, places = [], []
    for branch in pieces:
        found = []
        for array, low, n in branch:
            known = [i for i, other in enumerate(arrays) if other is array]
            if not known:
                known = [len(arrays)]
                arrays.append(array)
            found.append((known[0], low, n))
        places.append(found)
    return arrays, places


def branch_of(refs, places, head):
    return keys_and_values([refs[i] for i, _, _ in places], [(low, n) for _, low, n in places], head)


def attend(query, keys, values):
    scores = lax.dot_general(
        query, keys, (((1,), (1,)), ((), ())), preferred_element_type=F32
    )
    top = jnp.max(scores, axis=1, keepdims=True)
    probs = jnp.exp2((scores - top) * UNIT).astype(BF16)
    both = jnp.dot(probs, values, preferred_element_type=F32)
    top = jnp.broadcast_to(top * UNIT, (query.shape[0], HD))
    return top, both[:, HD:], both[:, :HD]


def merge(state, head, picked, found):
    top_ref, sum_ref, value_ref = state
    top, row_sum, value = found
    old = top_ref[head, picked, :]
    new = jnp.maximum(old, top)
    decay, weight = jnp.exp2(old - new), jnp.exp2(top - new)
    top_ref[head, picked, :] = new
    sum_ref[head, picked, :] = sum_ref[head, picked, :] * decay + row_sum * weight
    value_ref[head, picked, :] = value_ref[head, picked, :] * decay + value * weight


def compact_rows(branches, rows):
    return sum(rows >> b for b in branches)


def compact(state, head, picks, outs):
    low = 0
    for picked in picks:
        for ref, out in zip(state, outs):
            out[head, low : low + picked.size, :] = ref[head, picked, :]
        low += picked.size


def pick(offs, b, head, rows):
    return pl.ds(offs[b, head], rows >> b, stride=1 << b)


def early_kernel(count, places, parts, offs_hbm, tok, w_hbm, *refs):
    arrays, refs = refs[:count], refs[count:]
    outs, later_query, later = refs[:parts], refs[parts], refs[parts + 1 : parts + 4]
    offs, w_query, query, *state, sems = refs[parts + 4 :]
    heads, rows = query.shape[:2]
    part_rows = rows // parts
    me = lax.axis_index("head")
    copies = Copies(sems)
    loads = []
    for head in range(heads):
        source = w_hbm.at[:, pl.ds(head * 3 * HD, HD)]
        loads.append(copies.start(source, w_query.at[:, pl.ds(head * HD, HD)]))
    offs_load = copies.start(offs_hbm, offs)
    wait_all(loads)
    projected = jnp.dot(tok[...], w_query[...], preferred_element_type=F32).astype(BF16)
    step = min(rows, 256)
    offs_load.wait()
    for head in range(heads):
        mine = projected[:, head * HD : (head + 1) * HD]
        query[head] = mine.astype(F32)
        keys, values = branch_of(arrays, places[0], head)
        for low in range(0, rows, step):
            span = slice(low, low + step)
            for ref, array in zip(state, attend(mine[span], keys, values)):
                ref[head, span] = array
        keys, values = branch_of(arrays, places[1], head)
        picked = pick(offs, 1, me * heads + head, rows)
        merge(state, head, picked, attend(query[head, picked, :].astype(BF16), keys, values))
        _, row_sum, value = state
        columns = slice(head * HD, (head + 1) * HD)
        for d in range(parts):
            span = pl.ds(pl.multiple_of((me ^ d) * part_rows, part_rows), part_rows)
            outs[d][:, columns] = (value[head, span, :] / row_sum[head, span, :]).astype(BF16)
        picks = [pick(offs, b, me * heads + head, rows) for b in LATER]
        low = 0
        for picked in picks:
            later_query[head, low : low + picked.size, :] = query[head, picked, :].astype(BF16)
            low += picked.size
        compact(state, head, picks, later)


def early(offsets, tokens, w_qkv, pieces, parts):
    heads = w_qkv.shape[1] // (3 * HD)
    rows, width = tokens.shape
    arrays, places = operands(pieces)
    later = compact_rows(LATER, rows)
    out_shape = [shape(rows // parts, heads * HD)] * parts
    out_shape.append(shape(heads, later, HD))
    out_shape += [shape(heads, later, HD, dtype=F32)] * 3
    return pl.pallas_call(
        functools.partial(early_kernel, len(arrays), places, parts),
        in_specs=[HBM, VMEM, HBM] + [VMEM] * len(arrays),
        out_specs=[VMEM] * len(out_shape),
        out_shape=out_shape,
        scratch_shapes=[
            pltpu.SMEM(offsets.shape, jnp.int32),
            pltpu.VMEM((width, heads * HD), BF16),
            pltpu.VMEM((heads, rows, HD), F32),
            pltpu.VMEM((heads, rows, HD), F32),
            pltpu.VMEM((heads, rows, HD), F32),
            pltpu.VMEM((heads, rows, HD), F32),
            pltpu.SemaphoreType.DMA((1 + heads,)),
        ],
        compiler_params=pltpu.CompilerParams(vmem_limit_bytes=VMEM_LIMIT),
        cost_estimate=cost(4),
        name="early",
    )(in_hbm(offsets), tokens, in_hbm(w_qkv), *arrays)


def middle_kernel(count, places, parts, offs_hbm, query, top_in, sum_in, value_in, *refs):
    arrays, refs = refs[:count], refs[count:]
    outs, late_query, late = refs[:parts], refs[parts], refs[parts + 1 : parts + 4]
    offs, *state, sems = refs[parts + 4 :]
    _, row_sum, value = state
    heads, rows = value.shape[:2]
    part_rows = rows // parts
    me = lax.axis_index("head")
    offs_load = Copies(sems).start(offs_hbm, offs)
    (branch,) = MIDDLE
    own = rows >> branch
    found = []
    for head in range(heads):
        keys, values = branch_of(arrays, places[0], head)
        found.append(attend(query[head, :own, :], keys, values))
    offs_load.wait()
    for head in range(heads):
        picks = [pick(offs, b, me * heads + head, rows) for b in LATER]
        low = 0
        for picked in picks:
            for ref, array in zip(state, (top_in, sum_in, value_in)):
                ref[head, picked, :] = array[head, low : low + picked.size, :]
            low += picked.size
        merge(state, head, picks[0], found[head])
        for d in range(parts):
            start = (me ^ d) * part_rows + offs[branch, me * heads + head]
            source = pl.ds(start, part_rows >> branch, stride=1 << branch)
            outs[d][head] = (value[head, source, :] / row_sum[head, source, :]).astype(BF16)
        late_query[head] = query[head, own:, :]
        compact(state, head, picks[1:], late)


def middle(offsets, rows, query, state, pieces, parts):
    heads = query.shape[0]
    arrays, places = operands(pieces)
    late = compact_rows(LATE, rows)
    out_shape = [shape(heads, compact_rows(MIDDLE, rows // parts), HD)] * parts
    out_shape.append(shape(heads, late, HD))
    out_shape += [shape(heads, late, HD, dtype=F32)] * 3
    return pl.pallas_call(
        functools.partial(middle_kernel, len(arrays), places, parts),
        in_specs=[HBM] + [VMEM] * (4 + len(arrays)),
        out_specs=[VMEM] * len(out_shape),
        out_shape=out_shape,
        scratch_shapes=[
            pltpu.SMEM(offsets.shape, jnp.int32),
            pltpu.VMEM((heads, rows, HD), F32),
            pltpu.VMEM((heads, rows, HD), F32),
            pltpu.VMEM((heads, rows, HD), F32),
            pltpu.SemaphoreType.DMA((1,)),
        ],
        compiler_params=pltpu.CompilerParams(vmem_limit_bytes=VMEM_LIMIT),
        cost_estimate=cost(0.01),
        name="middle",
    )(in_hbm(offsets), query, *state, *arrays)


def joined_state(old, found):
    top = jnp.maximum(old[0], found[0])
    decay, weight = jnp.exp2(old[0] - top), jnp.exp2(found[0] - top)
    return top, *(a * decay + b * weight for a, b in zip(old[1:], found[1:]))


def late_kernel(count, places, parts, offs_hbm, query, *refs):
    state_in, arrays, refs = refs[:3], refs[3 : 3 + count], refs[3 + count :]
    before, outs, (offs, *state, ratio, chosen, sems) = refs[:parts], refs[parts : 2 * parts], refs[2 * parts :]
    heads, n3 = state[0].shape[:2]
    n4 = n3 // 2
    me = lax.axis_index("head")
    offs_load = Copies(sems).start(offs_hbm, offs)
    third, fourth = LATE
    found = []
    for head in range(heads):
        spans = (slice(0, n3), slice(n3, n3 + n4))
        for places_of, span in zip(places, spans):
            keys, values = branch_of(arrays, places_of, head)
            found.append(attend(query[head, span, :], keys, values))
    for head in range(heads):
        new = joined_state([ref[head, :n3, :] for ref in state_in], found[2 * head])
        for ref, array in zip(state, new):
            ref[head] = array
        ratio[head, :n3, :] = new[2] / new[1]
    offs_load.wait()
    for head in range(heads):
        offset = offs[fourth, me * heads + head]
        nested = (offset & ((1 << third) - 1)) == offs[third, me * heads + head]
        inner = pl.ds(offset >> third, n4, stride=2)
        old = [
            jnp.where(nested, ref[head, inner, :], given[head, n3:, :])
            for ref, given in zip(state, state_in)
        ]
        new = joined_state(old, found[2 * head + 1])
        ratio[head, n3:, :] = new[2] / new[1]
        for d in range(parts):
            low = 0
            for start, n in ((0, n3 // parts), (n3, n4 // parts)):
                chosen[low : low + n, :] = ratio[head, pl.ds(start + (me ^ d) * n, n), :]
                low += n
            known = before[d].shape[1]
            outs[d][head, :known] = before[d][head]
            outs[d][head, known:] = chosen[...].astype(BF16)


def late(offsets, rows, query, state, pieces, before):
    heads = query.shape[0]
    arrays, places = operands(pieces)
    parts = len(before)
    chosen = compact_rows(LATE, rows // parts)
    n3 = rows >> LATE[0]
    return pl.pallas_call(
        functools.partial(late_kernel, len(arrays), places, parts),
        in_specs=[HBM] + [VMEM] * (4 + len(arrays) + parts),
        out_specs=[VMEM] * parts,
        out_shape=[shape(heads, compact_rows(LATER, rows // parts), HD)] * parts,
        scratch_shapes=[
            pltpu.SMEM(offsets.shape, jnp.int32),
            pltpu.VMEM((heads, n3, HD), F32),
            pltpu.VMEM((heads, n3, HD), F32),
            pltpu.VMEM((heads, n3, HD), F32),
            pltpu.VMEM((heads, compact_rows(LATE, rows), HD), F32),
            pltpu.VMEM((chosen, HD), F32),
            pltpu.SemaphoreType.DMA((1,)),
        ],
        compiler_params=pltpu.CompilerParams(vmem_limit_bytes=VMEM_LIMIT),
        cost_estimate=cost(0.01),
        name="late",
    )(in_hbm(offsets), query, *state, *arrays, *before)


def mix_kernel(distances, heads, split, offs_hbm, *refs):
    count = len(distances)
    early_refs, later_refs, refs = refs[:count], refs[count : 2 * count], refs[2 * count :]
    total = None
    if refs[0].dtype == F32:
        total, refs = refs[0][...], refs[1:]
    w_refs, (out, offs, wide, narrow, joined, sems) = refs[:-6], refs[-6:]
    rows = out.shape[0]
    me = lax.axis_index("head")
    offs_load = Copies(sems).start(offs_hbm, offs)
    for i, d in enumerate(distances):
        for head in range(heads):
            wide[head] = early_refs[i][:, head * HD : (head + 1) * HD].astype(F32)
            narrow[head] = later_refs[i][head].astype(F32)
        if i == 0:
            offs_load.wait()
        for head in range(heads):
            low = 0
            for b in LATER:
                picked = pick(offs, b, (me ^ d) * heads + head, rows)
                wide[head, picked, :] = narrow[head, low : low + picked.size, :]
                low += picked.size
            joined[:, head * HD : (head + 1) * HD] = wide[head].astype(BF16)
        if split:
            part = lax.rem(lax.axis_index("seq"), 2)
            depth = w_refs[0].shape[0]
            columns = [pl.ds(pl.multiple_of((part ^ c) * depth, depth), depth) for c in range(2)]
            terms = [(joined[:, columns[c]], w_refs[c][...]) for c in range(2)]
        else:
            terms = [(joined[...], w_refs[i][...])]
        for left, right in terms:
            term = jnp.dot(left, right, preferred_element_type=F32)
            total = term if total is None else total + term
    out[...] = total.astype(out.dtype)


def mix(offsets, distances, early_parts, later_parts, weights, total, last):
    heads = later_parts[0].shape[0]
    rows, width = early_parts[0].shape[0], weights[0].shape[1]
    split = len(weights) > len(distances)
    totals = [] if total is None else [total]
    arrays = [*early_parts, *later_parts, *totals, *weights]
    return pl.pallas_call(
        functools.partial(mix_kernel, distances, heads, split),
        in_specs=[HBM] + [VMEM] * len(arrays),
        out_specs=VMEM,
        out_shape=shape(rows, width, dtype=BF16 if last else F32),
        scratch_shapes=[
            pltpu.SMEM(offsets.shape, jnp.int32),
            pltpu.VMEM((heads, rows, HD), F32),
            pltpu.VMEM((heads, compact_rows(LATER, rows), HD), F32),
            pltpu.VMEM((rows, heads * HD), BF16),
            pltpu.SemaphoreType.DMA((1,)),
        ],
        compiler_params=pltpu.CompilerParams(vmem_limit_bytes=VMEM_LIMIT),
        cost_estimate=cost(1),
        name="mix",
    )(in_hbm(offsets), *arrays)


def swap(x, axis, distance):
    return lax.ppermute(x, axis, [(i, i ^ distance) for i in range(lax.axis_size(axis))])


def together(arrays):
    return list(lax.optimization_barrier(tuple(arrays)))


def pair(piece):
    return [piece, swap(piece, "seq", 1)]


def layer_16(tokens, w_qkv, w_out, offsets):
    parts = lax.axis_size("head")
    rows = tokens.shape[0]
    n1, n2, n3, n4 = (rows >> b for b in range(1, NB))
    groups = [(1, 4, 3, 2), (4, 3, 2), (4, 3), (4,)]
    tokens, kv, near, all_own, far, b4, w_half = project(
        offsets, tokens, w_qkv, w_out, groups, True
    )
    near_core = swap(near, "seq", 1)
    b4_z8, b4_z12 = swap(b4, "seq", 8), swap(b4, "seq", 12)
    far_z4 = swap(far, "seq", 4)
    w_half = swap(w_half, "head", 1)
    all_y = swap(all_own, "seq", 2)
    nears = [near, near_core]
    pieces = [[(kv, 0, rows)], [(piece, 0, n1) for piece in nears]]
    first, other, query, *state = early(offsets, tokens, w_qkv, pieces, parts)
    all_y, far_z4, b4_z8, b4_z12, query = together([all_y, far_z4, b4_z8, b4_z12, query])
    b4_z = jnp.concatenate([b4_z8, b4_z12], axis=1)
    b4_yz = swap(b4_z, "seq", 2)
    far_yz4 = swap(all_y[:, : n4 + n3], "seq", 4)
    alls, far_z4s, b4_zs = pair(all_y), pair(far_z4), pair(b4_z)
    alls[1], far_z4s[1], b4_zs[1] = together([alls[1], far_z4s[1], b4_zs[1]])
    pieces = [
        [(piece, n1 + n4 + n3, n2) for piece in nears] + [(piece, n4 + n3, n2) for piece in alls]
    ]
    *middle_parts, query, top, row_sum, value = middle(
        offsets, rows, query, state, pieces, parts
    )
    state = [top, row_sum, value]
    other = swap(other, "head", 1)
    far_yz4, b4_yz, query = together([far_yz4, b4_yz, query])
    fars = alls + far_z4s + pair(far_yz4)
    b4_zs = b4_zs + pair(b4_yz)
    pieces = [
        [(piece, n1 + n4, n3) for piece in nears] + [(piece, n4, n3) for piece in fars],
        [(piece, n1, n4) for piece in nears]
        + [(piece, 0, n4) for piece in fars]
        + [(piece, 0, 2 * n4) for piece in b4_zs],
    ]
    late_parts = late(offsets, rows, query, state, pieces, middle_parts)
    w_half, other, *late_parts = together([w_half, other, *late_parts])
    late_part = swap(late_parts[1], "head", 1)
    total = mix(offsets, [0], [first], late_parts[:1], [w_out], None, False)
    weights = [w_half, swap(w_half, "seq", 1)]
    return mix(offsets, [1], [other], [late_part], weights, total, True)


def exchange(own, seq):
    gathered = []
    for b in range(NB):
        pieces = own[b]
        for step in range((seq * (1 << b) // 16).bit_length() - 1):
            pieces = jnp.concatenate([pieces, swap(pieces, "seq", 1 << step)], axis=1)
        gathered.append([(pieces, 0, pieces.shape[1])])
    return gathered


def on_device(tokens, w_qkv, w_out, offsets):
    seq, parts = lax.axis_size("seq"), lax.axis_size("head")
    rows = tokens.shape[0]
    if seq == 16 and parts == 2:
        return layer_16(tokens, w_qkv, w_out, offsets)
    groups = [(b,) for b in range(1, NB)]
    tokens, *own = project(offsets, tokens, w_qkv, w_out, groups, False)
    gathered = exchange(own, seq)
    weights = [w_out] + [swap(w_out, "head", d) for d in range(1, parts)]
    *early_parts, query, top, row_sum, value = early(
        offsets, tokens, w_qkv, gathered[:2], parts
    )
    state = [top, row_sum, value]
    *middle_parts, query, top, row_sum, value = middle(
        offsets, rows, query, state, gathered[2:3], parts
    )
    state = [top, row_sum, value]
    late_parts = list(late(offsets, rows, query, state, gathered[3:], middle_parts))
    for found in (early_parts, late_parts):
        found[1:] = [swap(found[d], "head", d) for d in range(1, parts)]
    return mix(offsets, list(range(parts)), early_parts, late_parts, weights, None, True)


def solution(mesh):
    in_specs = (P("seq", None), P(None, "head"), P("head", None), P())
    out_specs = P(("seq", "head"), None)
    return jax.shard_map(
        on_device, mesh=mesh, in_specs=in_specs, out_specs=out_specs, check_vma=False
    )
```

```python
import functools
import math

import jax
import jax.numpy as jnp
from jax import lax
from jax.experimental import pallas as pl
from jax.experimental.pallas import tpu as pltpu
from jax.sharding import PartitionSpec as P

HD = 128
NB = 5
MIDDLE, LATE = (2,), (3, 4)
LATER = MIDDLE + LATE
BF16 = jnp.bfloat16
F32 = jnp.float32
UNIT = math.log2(math.e) / math.sqrt(HD)
VMEM_LIMIT = 24 << 20
ANY = pl.BlockSpec(memory_space=pl.ANY)
VMEM = pl.BlockSpec(memory_space=pltpu.VMEM)
HBM = pl.BlockSpec(memory_space=pltpu.HBM)


def shape(*extent, dtype=BF16):
    return jax.ShapeDtypeStruct(extent, dtype)


class Copies:
    def __init__(self, sems):
        self.sems = sems
        self.used = 0

    def start(self, source, target):
        copy = pltpu.make_async_copy(source, target, self.sems.at[self.used])
        self.used += 1
        copy.start()
        return copy


def wait_all(copies):
    for copy in copies:
        copy.wait()


def in_hbm(x):
    return pltpu.with_memory_space_constraint(x, pltpu.HBM)


def cost(microseconds):
    return pl.CostEstimate(
        flops=int(microseconds * 1e9), bytes_accessed=0, transcendentals=0
    )


def project_kernel(groups, halves, offs_hbm, tok_hbm, w_hbm, wo_hbm, *refs):
    heads = w_hbm.shape[1] // (3 * HD)
    rows = tok_hbm.shape[0]
    outs, (offs, w, wide, sems) = refs[:-4], refs[-4:]
    tok, offs_out, outs = outs[0], outs[1], outs[2:]
    first = lax.axis_index("head") * heads
    copies = Copies(sems)
    loads = [copies.start(tok_hbm, tok)]
    for head in range(heads):
        columns = pl.ds(head * 3 * HD + HD, 2 * HD)
        target = w.at[:, pl.ds(head * 2 * HD, 2 * HD)]
        loads.append(copies.start(w_hbm.at[:, columns], target))
    offs_load = copies.start(offs_hbm, offs)
    stores = [copies.start(offs_hbm, offs_out)]
    if halves:
        depth = wo_hbm.shape[0] // 2
        part = lax.rem(lax.axis_index("seq"), 2)
        source = wo_hbm.at[pl.ds(pl.multiple_of(part * depth, depth), depth)]
        stores.append(copies.start(source, outs[-1]))
    loads[0].wait()
    step = min(heads, 2)
    for head in range(heads + 1):
        if head < heads and head % step == 0:
            wait_all(loads[head + 1 : head + 1 + step])
            columns = slice(head * 2 * HD, (head + step) * 2 * HD)
            both = jnp.dot(tok[...], w[:, columns], preferred_element_type=F32).astype(BF16)
            for i in range(2 * step):
                part = both[:, i * HD : (i + 1) * HD]
                outs[0][head + i // 2, :, i % 2 * HD : (i % 2 + 1) * HD] = part
                wide[2 * head + i] = part.astype(F32)
        if head == 0:
            offs_load.wait()
            continue
        done = head - 1
        for b in range(1, NB):
            n = rows >> b
            offset = offs[b, first + done]
            for c in range(2):
                picked = wide[2 * done + c, pl.ds(offset, n, stride=1 << b), :].astype(BF16)
                for out, group in zip(outs[1:], groups):
                    if b in group:
                        low = sum(rows >> other for other in group[: group.index(b)])
                        out[done, low : low + n, c * HD : (c + 1) * HD] = picked
    wait_all(stores)


def project(offsets, tokens, w_qkv, w_out, groups, halves):
    heads = w_qkv.shape[1] // (3 * HD)
    rows, width = tokens.shape
    out_shape = [shape(rows, width), shape(*offsets.shape, dtype=jnp.int32)]
    out_shape.append(shape(heads, rows, 2 * HD))
    for group in groups:
        out_shape.append(shape(heads, sum(rows >> b for b in group), 2 * HD))
    out_specs = [VMEM] * len(out_shape)
    if halves:
        out_shape.append(shape(w_out.shape[0] // 2, w_out.shape[1]))
        out_specs.append(ANY)
    return pl.pallas_call(
        functools.partial(project_kernel, groups, halves),
        in_specs=[HBM, HBM, HBM, HBM],
        out_specs=out_specs,
        out_shape=out_shape,
        scratch_shapes=[
            pltpu.SMEM(offsets.shape, jnp.int32),
            pltpu.VMEM((width, heads * 2 * HD), BF16),
            pltpu.VMEM((2 * heads, rows, HD), F32),
            pltpu.SemaphoreType.DMA((4 + heads,)),
        ],
        compiler_params=pltpu.CompilerParams(vmem_limit_bytes=VMEM_LIMIT),
        cost_estimate=cost(5),
        name="project",
    )(in_hbm(offsets), in_hbm(tokens), in_hbm(w_qkv), in_hbm(w_out))


def keys_and_values(refs, spans, head):
    parts = [ref[head, low : low + n, :] for ref, (low, n) in zip(refs, spans)]
    both = jnp.concatenate(parts, axis=0) if len(parts) > 1 else parts[0]
    ones = jnp.ones((both.shape[0], HD), BF16)
    return both[:, :HD], jnp.concatenate([both[:, HD:], ones], axis=1)


def operands(pieces):
    arrays, places = [], []
    for branch in pieces:
        found = []
        for array, low, n in branch:
            known = [i for i, other in enumerate(arrays) if other is array]
            if not known:
                known = [len(arrays)]
                arrays.append(array)
            found.append((known[0], low, n))
        places.append(found)
    return arrays, places


def branch_of(refs, places, head):
    return keys_and_values([refs[i] for i, _, _ in places], [(low, n) for _, low, n in places], head)


def attend(query, keys, values):
    scores = lax.dot_general(
        query, keys, (((1,), (1,)), ((), ())), preferred_element_type=F32
    )
    top = jnp.max(scores, axis=1, keepdims=True)
    probs = jnp.exp2((scores - top) * UNIT).astype(BF16)
    both = jnp.dot(probs, values, preferred_element_type=F32)
    top = jnp.broadcast_to(top * UNIT, (query.shape[0], HD))
    return top, both[:, HD:], both[:, :HD]


def merge(state, head, picked, found):
    top_ref, sum_ref, value_ref = state
    top, row_sum, value = found
    old = top_ref[head, picked, :]
    new = jnp.maximum(old, top)
    decay, weight = jnp.exp2(old - new), jnp.exp2(top - new)
    top_ref[head, picked, :] = new
    sum_ref[head, picked, :] = sum_ref[head, picked, :] * decay + row_sum * weight
    value_ref[head, picked, :] = value_ref[head, picked, :] * decay + value * weight


def compact_rows(branches, rows):
    return sum(rows >> b for b in branches)


def compact(state, head, picks, outs):
    low = 0
    for picked in picks:
        for ref, out in zip(state, outs):
            out[head, low : low + picked.size, :] = ref[head, picked, :]
        low += picked.size


def pick(offs, b, head, rows):
    return pl.ds(offs[b, head], rows >> b, stride=1 << b)


def early_kernel(count, places, parts, offs_hbm, tok, w_hbm, *refs):
    arrays, refs = refs[:count], refs[count:]
    outs, later_query, later = refs[:parts], refs[parts], refs[parts + 1 : parts + 4]
    offs, w_query, query, *state, sems = refs[parts + 4 :]
    heads, rows = query.shape[:2]
    part_rows = rows // parts
    me = lax.axis_index("head")
    copies = Copies(sems)
    loads = []
    for head in range(heads):
        source = w_hbm.at[:, pl.ds(head * 3 * HD, HD)]
        loads.append(copies.start(source, w_query.at[:, pl.ds(head * HD, HD)]))
    offs_load = copies.start(offs_hbm, offs)
    wait_all(loads)
    projected = jnp.dot(tok[...], w_query[...], preferred_element_type=F32).astype(BF16)
    step = min(rows, 256)
    offs_load.wait()
    for head in range(heads):
        mine = projected[:, head * HD : (head + 1) * HD]
        query[head] = mine.astype(F32)
        keys, values = branch_of(arrays, places[0], head)
        for low in range(0, rows, step):
            span = slice(low, low + step)
            for ref, array in zip(state, attend(mine[span], keys, values)):
                ref[head, span] = array
        keys, values = branch_of(arrays, places[1], head)
        picked = pick(offs, 1, me * heads + head, rows)
        merge(state, head, picked, attend(query[head, picked, :].astype(BF16), keys, values))
        _, row_sum, value = state
        columns = slice(head * HD, (head + 1) * HD)
        for d in range(parts):
            span = pl.ds(pl.multiple_of((me ^ d) * part_rows, part_rows), part_rows)
            outs[d][:, columns] = (value[head, span, :] / row_sum[head, span, :]).astype(BF16)
        picks = [pick(offs, b, me * heads + head, rows) for b in LATER]
        low = 0
        for picked in picks:
            later_query[head, low : low + picked.size, :] = query[head, picked, :].astype(BF16)
            low += picked.size
        compact(state, head, picks, later)


def early(offsets, tokens, w_qkv, pieces, parts):
    heads = w_qkv.shape[1] // (3 * HD)
    rows, width = tokens.shape
    arrays, places = operands(pieces)
    later = compact_rows(LATER, rows)
    out_shape = [shape(rows // parts, heads * HD)] * parts
    out_shape.append(shape(heads, later, HD))
    out_shape += [shape(heads, later, HD, dtype=F32)] * 3
    return pl.pallas_call(
        functools.partial(early_kernel, len(arrays), places, parts),
        in_specs=[HBM, VMEM, HBM] + [VMEM] * len(arrays),
        out_specs=[VMEM] * len(out_shape),
        out_shape=out_shape,
        scratch_shapes=[
            pltpu.SMEM(offsets.shape, jnp.int32),
            pltpu.VMEM((width, heads * HD), BF16),
            pltpu.VMEM((heads, rows, HD), F32),
            pltpu.VMEM((heads, rows, HD), F32),
            pltpu.VMEM((heads, rows, HD), F32),
            pltpu.VMEM((heads, rows, HD), F32),
            pltpu.SemaphoreType.DMA((1 + heads,)),
        ],
        compiler_params=pltpu.CompilerParams(vmem_limit_bytes=VMEM_LIMIT),
        cost_estimate=cost(4),
        name="early",
    )(in_hbm(offsets), tokens, in_hbm(w_qkv), *arrays)


def middle_kernel(count, places, parts, offs_hbm, query, top_in, sum_in, value_in, *refs):
    arrays, refs = refs[:count], refs[count:]
    outs, late_query, late = refs[:parts], refs[parts], refs[parts + 1 : parts + 4]
    offs, *state, sems = refs[parts + 4 :]
    _, row_sum, value = state
    heads, rows = value.shape[:2]
    part_rows = rows // parts
    me = lax.axis_index("head")
    offs_load = Copies(sems).start(offs_hbm, offs)
    (branch,) = MIDDLE
    own = rows >> branch
    found = []
    for head in range(heads):
        keys, values = branch_of(arrays, places[0], head)
        found.append(attend(query[head, :own, :], keys, values))
    offs_load.wait()
    for head in range(heads):
        picks = [pick(offs, b, me * heads + head, rows) for b in LATER]
        low = 0
        for picked in picks:
            for ref, array in zip(state, (top_in, sum_in, value_in)):
                ref[head, picked, :] = array[head, low : low + picked.size, :]
            low += picked.size
        merge(state, head, picks[0], found[head])
        for d in range(parts):
            start = (me ^ d) * part_rows + offs[branch, me * heads + head]
            source = pl.ds(start, part_rows >> branch, stride=1 << branch)
            outs[d][head] = (value[head, source, :] / row_sum[head, source, :]).astype(BF16)
        late_query[head] = query[head, own:, :]
        compact(state, head, picks[1:], late)


def middle(offsets, rows, query, state, pieces, parts):
    heads = query.shape[0]
    arrays, places = operands(pieces)
    late = compact_rows(LATE, rows)
    out_shape = [shape(heads, compact_rows(MIDDLE, rows // parts), HD)] * parts
    out_shape.append(shape(heads, late, HD))
    out_shape += [shape(heads, late, HD, dtype=F32)] * 3
    return pl.pallas_call(
        functools.partial(middle_kernel, len(arrays), places, parts),
        in_specs=[HBM] + [VMEM] * (4 + len(arrays)),
        out_specs=[VMEM] * len(out_shape),
        out_shape=out_shape,
        scratch_shapes=[
            pltpu.SMEM(offsets.shape, jnp.int32),
            pltpu.VMEM((heads, rows, HD), F32),
            pltpu.VMEM((heads, rows, HD), F32),
            pltpu.VMEM((heads, rows, HD), F32),
            pltpu.SemaphoreType.DMA((1,)),
        ],
        compiler_params=pltpu.CompilerParams(vmem_limit_bytes=VMEM_LIMIT),
        cost_estimate=cost(0.01),
        name="middle",
    )(in_hbm(offsets), query, *state, *arrays)


def joined_state(old, found):
    top = jnp.maximum(old[0], found[0])
    decay, weight = jnp.exp2(old[0] - top), jnp.exp2(found[0] - top)
    return top, *(a * decay + b * weight for a, b in zip(old[1:], found[1:]))


def late_kernel(count, places, parts, offs_hbm, query, *refs):
    state_in, arrays, refs = refs[:3], refs[3 : 3 + count], refs[3 + count :]
    before, outs, (offs, *state, ratio, chosen, sems) = refs[:parts], refs[parts : 2 * parts], refs[2 * parts :]
    heads, n3 = state[0].shape[:2]
    n4 = n3 // 2
    me = lax.axis_index("head")
    offs_load = Copies(sems).start(offs_hbm, offs)
    third, fourth = LATE
    found = []
    for head in range(heads):
        spans = (slice(0, n3), slice(n3, n3 + n4))
        for places_of, span in zip(places, spans):
            keys, values = branch_of(arrays, places_of, head)
            found.append(attend(query[head, span, :], keys, values))
    for head in range(heads):
        new = joined_state([ref[head, :n3, :] for ref in state_in], found[2 * head])
        for ref, array in zip(state, new):
            ref[head] = array
        ratio[head, :n3, :] = new[2] / new[1]
    offs_load.wait()
    for head in range(heads):
        offset = offs[fourth, me * heads + head]
        nested = (offset & ((1 << third) - 1)) == offs[third, me * heads + head]
        inner = pl.ds(offset >> third, n4, stride=2)
        old = [
            jnp.where(nested, ref[head, inner, :], given[head, n3:, :])
            for ref, given in zip(state, state_in)
        ]
        new = joined_state(old, found[2 * head + 1])
        ratio[head, n3:, :] = new[2] / new[1]
        for d in range(parts):
            low = 0
            for start, n in ((0, n3 // parts), (n3, n4 // parts)):
                chosen[low : low + n, :] = ratio[head, pl.ds(start + (me ^ d) * n, n), :]
                low += n
            known = before[d].shape[1]
            outs[d][head, :known] = before[d][head]
            outs[d][head, known:] = chosen[...].astype(BF16)


def late(offsets, rows, query, state, pieces, before):
    heads = query.shape[0]
    arrays, places = operands(pieces)
    parts = len(before)
    chosen = compact_rows(LATE, rows // parts)
    n3 = rows >> LATE[0]
    return pl.pallas_call(
        functools.partial(late_kernel, len(arrays), places, parts),
        in_specs=[HBM] + [VMEM] * (4 + len(arrays) + parts),
        out_specs=[VMEM] * parts,
        out_shape=[shape(heads, compact_rows(LATER, rows // parts), HD)] * parts,
        scratch_shapes=[
            pltpu.SMEM(offsets.shape, jnp.int32),
            pltpu.VMEM((heads, n3, HD), F32),
            pltpu.VMEM((heads, n3, HD), F32),
            pltpu.VMEM((heads, n3, HD), F32),
            pltpu.VMEM((heads, compact_rows(LATE, rows), HD), F32),
            pltpu.VMEM((chosen, HD), F32),
            pltpu.SemaphoreType.DMA((1,)),
        ],
        compiler_params=pltpu.CompilerParams(vmem_limit_bytes=VMEM_LIMIT),
        cost_estimate=cost(0.01),
        name="late",
    )(in_hbm(offsets), query, *state, *arrays, *before)


def mix_kernel(distances, heads, split, offs_in, *refs):
    count = len(distances)
    early_refs, later_refs, refs = refs[:count], refs[count : 2 * count], refs[2 * count :]
    total = None
    if refs[0].dtype == F32:
        total, refs = refs[0][...], refs[1:]
    w_refs, (out, offs, wide, narrow, joined, sems) = refs[:-6], refs[-6:]
    rows = out.shape[0]
    me = lax.axis_index("head")
    offs_load = Copies(sems).start(offs_in, offs)
    for i, d in enumerate(distances):
        for head in range(heads):
            wide[head] = early_refs[i][:, head * HD : (head + 1) * HD].astype(F32)
            narrow[head] = later_refs[i][head].astype(F32)
        if i == 0:
            offs_load.wait()
        for head in range(heads):
            low = 0
            for b in LATER:
                picked = pick(offs, b, (me ^ d) * heads + head, rows)
                wide[head, picked, :] = narrow[head, low : low + picked.size, :]
                low += picked.size
            joined[:, head * HD : (head + 1) * HD] = wide[head].astype(BF16)
        if split:
            part = lax.rem(lax.axis_index("seq"), 2)
            depth = w_refs[0].shape[0]
            columns = [pl.ds(pl.multiple_of((part ^ c) * depth, depth), depth) for c in range(2)]
            terms = [(joined[:, columns[c]], w_refs[c][...]) for c in range(2)]
        else:
            terms = [(joined[...], w_refs[i][...])]
        for left, right in terms:
            term = jnp.dot(left, right, preferred_element_type=F32)
            total = term if total is None else total + term
    out[...] = total.astype(out.dtype)


def mix(offsets, distances, early_parts, later_parts, weights, total, last):
    heads = later_parts[0].shape[0]
    rows, width = early_parts[0].shape[0], weights[0].shape[1]
    split = len(weights) > len(distances)
    totals = [] if total is None else [total]
    arrays = [*early_parts, *later_parts, *totals, *weights]
    return pl.pallas_call(
        functools.partial(mix_kernel, distances, heads, split),
        in_specs=[VMEM] * (1 + len(arrays)),
        out_specs=VMEM,
        out_shape=shape(rows, width, dtype=BF16 if last else F32),
        scratch_shapes=[
            pltpu.SMEM(offsets.shape, jnp.int32),
            pltpu.VMEM((heads, rows, HD), F32),
            pltpu.VMEM((heads, compact_rows(LATER, rows), HD), F32),
            pltpu.VMEM((rows, heads * HD), BF16),
            pltpu.SemaphoreType.DMA((1,)),
        ],
        compiler_params=pltpu.CompilerParams(vmem_limit_bytes=VMEM_LIMIT),
        cost_estimate=cost(1),
        name="mix",
    )(offsets, *arrays)


def swap(x, axis, distance):
    return lax.ppermute(x, axis, [(i, i ^ distance) for i in range(lax.axis_size(axis))])


def together(arrays):
    return list(lax.optimization_barrier(tuple(arrays)))


def pair(piece):
    return [piece, swap(piece, "seq", 1)]


def layer_16(tokens, w_qkv, w_out, offsets):
    parts = lax.axis_size("head")
    rows = tokens.shape[0]
    n1, n2, n3, n4 = (rows >> b for b in range(1, NB))
    groups = [(1, 4, 3, 2), (4, 3, 2), (4, 3), (4,)]
    tokens, near_offsets, kv, near, all_own, far, b4, w_half = project(
        offsets, tokens, w_qkv, w_out, groups, True
    )
    near_core = swap(near, "seq", 1)
    b4_z8, b4_z12 = swap(b4, "seq", 8), swap(b4, "seq", 12)
    far_z4 = swap(far, "seq", 4)
    w_half = swap(w_half, "head", 1)
    all_y = swap(all_own, "seq", 2)
    nears = [near, near_core]
    pieces = [[(kv, 0, rows)], [(piece, 0, n1) for piece in nears]]
    first, other, query, *state = early(offsets, tokens, w_qkv, pieces, parts)
    all_y, far_z4, b4_z8, b4_z12, query = together([all_y, far_z4, b4_z8, b4_z12, query])
    b4_z = jnp.concatenate([b4_z8, b4_z12], axis=1)
    b4_yz = swap(b4_z, "seq", 2)
    far_yz4 = swap(all_y[:, : n4 + n3], "seq", 4)
    alls, far_z4s, b4_zs = pair(all_y), pair(far_z4), pair(b4_z)
    alls[1], far_z4s[1], b4_zs[1] = together([alls[1], far_z4s[1], b4_zs[1]])
    pieces = [
        [(piece, n1 + n4 + n3, n2) for piece in nears] + [(piece, n4 + n3, n2) for piece in alls]
    ]
    *middle_parts, query, top, row_sum, value = middle(
        offsets, rows, query, state, pieces, parts
    )
    state = [top, row_sum, value]
    other = swap(other, "head", 1)
    far_yz4, b4_yz, query = together([far_yz4, b4_yz, query])
    fars = alls + far_z4s + pair(far_yz4)
    b4_zs = b4_zs + pair(b4_yz)
    pieces = [
        [(piece, n1 + n4, n3) for piece in nears] + [(piece, n4, n3) for piece in fars],
        [(piece, n1, n4) for piece in nears]
        + [(piece, 0, n4) for piece in fars]
        + [(piece, 0, 2 * n4) for piece in b4_zs],
    ]
    late_parts = late(offsets, rows, query, state, pieces, middle_parts)
    w_half, other, *late_parts = together([w_half, other, *late_parts])
    late_part = swap(late_parts[1], "head", 1)
    total = mix(near_offsets, [0], [first], late_parts[:1], [w_out], None, False)
    weights = [w_half, swap(w_half, "seq", 1)]
    return mix(near_offsets, [1], [other], [late_part], weights, total, True)


def exchange(own, seq):
    gathered = []
    for b in range(NB):
        pieces = own[b]
        for step in range((seq * (1 << b) // 16).bit_length() - 1):
            pieces = jnp.concatenate([pieces, swap(pieces, "seq", 1 << step)], axis=1)
        gathered.append([(pieces, 0, pieces.shape[1])])
    return gathered


def on_device(tokens, w_qkv, w_out, offsets):
    seq, parts = lax.axis_size("seq"), lax.axis_size("head")
    rows = tokens.shape[0]
    if seq == 16 and parts == 2:
        return layer_16(tokens, w_qkv, w_out, offsets)
    groups = [(b,) for b in range(1, NB)]
    tokens, near_offsets, *own = project(offsets, tokens, w_qkv, w_out, groups, False)
    gathered = exchange(own, seq)
    weights = [w_out] + [swap(w_out, "head", d) for d in range(1, parts)]
    *early_parts, query, top, row_sum, value = early(
        offsets, tokens, w_qkv, gathered[:2], parts
    )
    state = [top, row_sum, value]
    *middle_parts, query, top, row_sum, value = middle(
        offsets, rows, query, state, gathered[2:3], parts
    )
    state = [top, row_sum, value]
    late_parts = list(late(offsets, rows, query, state, gathered[3:], middle_parts))
    for found in (early_parts, late_parts):
        found[1:] = [swap(found[d], "head", d) for d in range(1, parts)]
    return mix(near_offsets, list(range(parts)), early_parts, late_parts, weights, None, True)


def solution(mesh):
    in_specs = (P("seq", None), P(None, "head"), P("head", None), P())
    out_specs = P(("seq", "head"), None)
    return jax.shard_map(
        on_device, mesh=mesh, in_specs=in_specs, out_specs=out_specs, check_vma=False
    )
```

```python
import functools
import math

import jax
import jax.numpy as jnp
from jax import lax
from jax.experimental import pallas as pl
from jax.experimental.pallas import tpu as pltpu
from jax.sharding import PartitionSpec as P

HD = 128
NB = 5
MIDDLE, LATE = (2,), (3, 4)
LATER = MIDDLE + LATE
BF16 = jnp.bfloat16
F32 = jnp.float32
UNIT = math.log2(math.e) / math.sqrt(HD)
VMEM_LIMIT = 24 << 20
CHUNKS = 2
ANY = pl.BlockSpec(memory_space=pl.ANY)
VMEM = pl.BlockSpec(memory_space=pltpu.VMEM)
HBM = pl.BlockSpec(memory_space=pltpu.HBM)


def shape(*extent, dtype=BF16):
    return jax.ShapeDtypeStruct(extent, dtype)


class Copies:
    def __init__(self, sems):
        self.sems = sems
        self.used = 0

    def start(self, source, target):
        copy = pltpu.make_async_copy(source, target, self.sems.at[self.used])
        self.used += 1
        copy.start()
        return copy


def wait_all(copies):
    for copy in copies:
        copy.wait()


def in_hbm(x):
    return pltpu.with_memory_space_constraint(x, pltpu.HBM)


def cost(microseconds):
    return pl.CostEstimate(
        flops=int(microseconds * 1e9), bytes_accessed=0, transcendentals=0
    )


def project_kernel(groups, halves, offs_hbm, tok_hbm, w_hbm, wo_hbm, *refs):
    heads = w_hbm.shape[1] // (3 * HD)
    rows = tok_hbm.shape[0]
    outs, (offs, w, wide, sems) = refs[:-4], refs[-4:]
    tok, offs_out, outs = outs[0], outs[1], outs[2:]
    first = lax.axis_index("head") * heads
    copies = Copies(sems)
    step = min(heads, 2)
    half = tok.shape[1] // 2
    tok_loads, loads = [], []
    for low in (0, half):
        depth = pl.ds(low, half)
        tok_loads.append(copies.start(tok_hbm.at[:, depth], tok.at[:, depth]))
        for head in range(step):
            source = w_hbm.at[depth, pl.ds(head * 3 * HD + HD, 2 * HD)]
            loads.append(copies.start(source, w.at[depth, pl.ds(head * 2 * HD, 2 * HD)]))
    for head in range(step, heads):
        columns = pl.ds(head * 3 * HD + HD, 2 * HD)
        loads.append(copies.start(w_hbm.at[:, columns], w.at[:, pl.ds(head * 2 * HD, 2 * HD)]))
    offs_load = copies.start(offs_hbm, offs)
    stores = [copies.start(offs_hbm, offs_out)]
    if halves:
        depth = wo_hbm.shape[0] // 2
        part = lax.rem(lax.axis_index("seq"), 2)
        source = wo_hbm.at[pl.ds(pl.multiple_of(part * depth, depth), depth)]
        stores.append(copies.start(source, outs[-1]))
    for head in range(heads + 1):
        if head < heads and head % step == 0:
            columns = slice(head * 2 * HD, (head + step) * 2 * HD)
            if head == 0:
                both = None
                for i, low in enumerate((0, half)):
                    tok_loads[i].wait()
                    wait_all(loads[i * step : (i + 1) * step])
                    term = jnp.dot(
                        tok[:, low : low + half],
                        w[low : low + half, columns],
                        preferred_element_type=F32,
                    )
                    both = term if both is None else both + term
            else:
                wait_all(loads[head + step : head + 2 * step])
                both = jnp.dot(tok[...], w[:, columns], preferred_element_type=F32)
            both = both.astype(BF16)
            for i in range(2 * step):
                part = both[:, i * HD : (i + 1) * HD]
                outs[0][head + i // 2, :, i % 2 * HD : (i % 2 + 1) * HD] = part
                wide[2 * head + i] = part.astype(F32)
        if head == 0:
            offs_load.wait()
            continue
        done = head - 1
        for b in range(1, NB):
            n = rows >> b
            offset = offs[b, first + done]
            for c in range(2):
                picked = wide[2 * done + c, pl.ds(offset, n, stride=1 << b), :].astype(BF16)
                for out, group in zip(outs[1:], groups):
                    if b in group:
                        low = sum(rows >> other for other in group[: group.index(b)])
                        out[done, low : low + n, c * HD : (c + 1) * HD] = picked
    wait_all(stores)


def project(offsets, tokens, w_qkv, w_out, groups, halves):
    heads = w_qkv.shape[1] // (3 * HD)
    rows, width = tokens.shape
    out_shape = [shape(rows, width), shape(*offsets.shape, dtype=jnp.int32)]
    out_shape.append(shape(heads, rows, 2 * HD))
    for group in groups:
        out_shape.append(shape(heads, sum(rows >> b for b in group), 2 * HD))
    out_specs = [VMEM] * len(out_shape)
    if halves:
        out_shape.append(shape(w_out.shape[0] // 2, w_out.shape[1]))
        out_specs.append(ANY)
    return pl.pallas_call(
        functools.partial(project_kernel, groups, halves),
        in_specs=[HBM, HBM, HBM, HBM],
        out_specs=out_specs,
        out_shape=out_shape,
        scratch_shapes=[
            pltpu.SMEM(offsets.shape, jnp.int32),
            pltpu.VMEM((width, heads * 2 * HD), BF16),
            pltpu.VMEM((2 * heads, rows, HD), F32),
            pltpu.SemaphoreType.DMA((7 + heads,)),
        ],
        compiler_params=pltpu.CompilerParams(vmem_limit_bytes=VMEM_LIMIT),
        cost_estimate=cost(5),
        name="project",
    )(in_hbm(offsets), in_hbm(tokens), in_hbm(w_qkv), in_hbm(w_out))


def keys_and_values(refs, spans, head):
    parts = [ref[head, low : low + n, :] for ref, (low, n) in zip(refs, spans)]
    both = jnp.concatenate(parts, axis=0) if len(parts) > 1 else parts[0]
    ones = jnp.ones((both.shape[0], HD), BF16)
    return both[:, :HD], jnp.concatenate([both[:, HD:], ones], axis=1)


def operands(pieces):
    arrays, places = [], []
    for branch in pieces:
        found = []
        for array, low, n in branch:
            known = [i for i, other in enumerate(arrays) if other is array]
            if not known:
                known = [len(arrays)]
                arrays.append(array)
            found.append((known[0], low, n))
        places.append(found)
    return arrays, places


def branch_of(refs, places, head):
    return keys_and_values([refs[i] for i, _, _ in places], [(low, n) for _, low, n in places], head)


def attend(query, keys, values):
    scores = lax.dot_general(
        query, keys, (((1,), (1,)), ((), ())), preferred_element_type=F32
    )
    top = jnp.max(scores, axis=1, keepdims=True)
    probs = jnp.exp2((scores - top) * UNIT).astype(BF16)
    both = jnp.dot(probs, values, preferred_element_type=F32)
    top = jnp.broadcast_to(top * UNIT, (query.shape[0], HD))
    return top, both[:, HD:], both[:, :HD]


def merge(state, head, picked, found):
    top_ref, sum_ref, value_ref = state
    top, row_sum, value = found
    old = top_ref[head, picked, :]
    new = jnp.maximum(old, top)
    decay, weight = jnp.exp2(old - new), jnp.exp2(top - new)
    top_ref[head, picked, :] = new
    sum_ref[head, picked, :] = sum_ref[head, picked, :] * decay + row_sum * weight
    value_ref[head, picked, :] = value_ref[head, picked, :] * decay + value * weight


def compact_rows(branches, rows):
    return sum(rows >> b for b in branches)


def compact(state, head, picks, outs):
    low = 0
    for picked in picks:
        for ref, out in zip(state, outs):
            out[head, low : low + picked.size, :] = ref[head, picked, :]
        low += picked.size


def pick(offs, b, head, rows):
    return pl.ds(offs[b, head], rows >> b, stride=1 << b)


def early_kernel(count, places, parts, offs_hbm, tok, w_hbm, *refs):
    arrays, refs = refs[:count], refs[count:]
    outs, later_query, later = refs[:parts], refs[parts], refs[parts + 1 : parts + 4]
    offs, w_query, query, *state, sems = refs[parts + 4 :]
    heads, rows = query.shape[:2]
    part_rows = rows // parts
    me = lax.axis_index("head")
    copies = Copies(sems)
    loads = []
    for head in range(heads):
        source = w_hbm.at[:, pl.ds(head * 3 * HD, HD)]
        loads.append(copies.start(source, w_query.at[:, pl.ds(head * HD, HD)]))
    offs_load = copies.start(offs_hbm, offs)
    wait_all(loads)
    projected = jnp.dot(tok[...], w_query[...], preferred_element_type=F32).astype(BF16)
    step = min(rows, 256)
    offs_load.wait()
    for head in range(heads):
        mine = projected[:, head * HD : (head + 1) * HD]
        query[head] = mine.astype(F32)
        keys, values = branch_of(arrays, places[0], head)
        for low in range(0, rows, step):
            span = slice(low, low + step)
            for ref, array in zip(state, attend(mine[span], keys, values)):
                ref[head, span] = array
        keys, values = branch_of(arrays, places[1], head)
        picked = pick(offs, 1, me * heads + head, rows)
        merge(state, head, picked, attend(query[head, picked, :].astype(BF16), keys, values))
        _, row_sum, value = state
        columns = slice(head * HD, (head + 1) * HD)
        for d in range(parts):
            span = pl.ds(pl.multiple_of((me ^ d) * part_rows, part_rows), part_rows)
            outs[d][:, columns] = (value[head, span, :] / row_sum[head, span, :]).astype(BF16)
        picks = [pick(offs, b, me * heads + head, rows) for b in LATER]
        low = 0
        for picked in picks:
            later_query[head, low : low + picked.size, :] = query[head, picked, :].astype(BF16)
            low += picked.size
        compact(state, head, picks, later)


def early(offsets, tokens, w_qkv, pieces, parts):
    heads = w_qkv.shape[1] // (3 * HD)
    rows, width = tokens.shape
    arrays, places = operands(pieces)
    later = compact_rows(LATER, rows)
    out_shape = [shape(rows // parts, heads * HD)] * parts
    out_shape.append(shape(heads, later, HD))
    out_shape += [shape(heads, later, HD, dtype=F32)] * 3
    return pl.pallas_call(
        functools.partial(early_kernel, len(arrays), places, parts),
        in_specs=[HBM, VMEM, HBM] + [VMEM] * len(arrays),
        out_specs=[VMEM] * len(out_shape),
        out_shape=out_shape,
        scratch_shapes=[
            pltpu.SMEM(offsets.shape, jnp.int32),
            pltpu.VMEM((width, heads * HD), BF16),
            pltpu.VMEM((heads, rows, HD), F32),
            pltpu.VMEM((heads, rows, HD), F32),
            pltpu.VMEM((heads, rows, HD), F32),
            pltpu.VMEM((heads, rows, HD), F32),
            pltpu.SemaphoreType.DMA((1 + heads,)),
        ],
        compiler_params=pltpu.CompilerParams(vmem_limit_bytes=VMEM_LIMIT),
        cost_estimate=cost(4),
        name="early",
    )(in_hbm(offsets), tokens, in_hbm(w_qkv), *arrays)


def middle_kernel(count, places, parts, offs_hbm, query, top_in, sum_in, value_in, *refs):
    arrays, refs = refs[:count], refs[count:]
    outs, late_query, late = refs[:parts], refs[parts], refs[parts + 1 : parts + 4]
    offs, *state, sems = refs[parts + 4 :]
    _, row_sum, value = state
    heads, rows = value.shape[:2]
    part_rows = rows // parts
    me = lax.axis_index("head")
    offs_load = Copies(sems).start(offs_hbm, offs)
    (branch,) = MIDDLE
    own = rows >> branch
    found = []
    for head in range(heads):
        keys, values = branch_of(arrays, places[0], head)
        found.append(attend(query[head, :own, :], keys, values))
    offs_load.wait()
    for head in range(heads):
        picks = [pick(offs, b, me * heads + head, rows) for b in LATER]
        low = 0
        for picked in picks:
            for ref, array in zip(state, (top_in, sum_in, value_in)):
                ref[head, picked, :] = array[head, low : low + picked.size, :]
            low += picked.size
        merge(state, head, picks[0], found[head])
        for d in range(parts):
            start = (me ^ d) * part_rows + offs[branch, me * heads + head]
            source = pl.ds(start, part_rows >> branch, stride=1 << branch)
            outs[d][head] = (value[head, source, :] / row_sum[head, source, :]).astype(BF16)
        late_query[head] = query[head, own:, :]
        compact(state, head, picks[1:], late)


def middle(offsets, rows, query, state, pieces, parts):
    heads = query.shape[0]
    arrays, places = operands(pieces)
    late = compact_rows(LATE, rows)
    out_shape = [shape(heads, compact_rows(MIDDLE, rows // parts), HD)] * parts
    out_shape.append(shape(heads, late, HD))
    out_shape += [shape(heads, late, HD, dtype=F32)] * 3
    return pl.pallas_call(
        functools.partial(middle_kernel, len(arrays), places, parts),
        in_specs=[HBM] + [VMEM] * (4 + len(arrays)),
        out_specs=[VMEM] * len(out_shape),
        out_shape=out_shape,
        scratch_shapes=[
            pltpu.SMEM(offsets.shape, jnp.int32),
            pltpu.VMEM((heads, rows, HD), F32),
            pltpu.VMEM((heads, rows, HD), F32),
            pltpu.VMEM((heads, rows, HD), F32),
            pltpu.SemaphoreType.DMA((1,)),
        ],
        compiler_params=pltpu.CompilerParams(vmem_limit_bytes=VMEM_LIMIT),
        cost_estimate=cost(0.01),
        name="middle",
    )(in_hbm(offsets), query, *state, *arrays)


def joined_state(old, found):
    top = jnp.maximum(old[0], found[0])
    decay, weight = jnp.exp2(old[0] - top), jnp.exp2(found[0] - top)
    return top, *(a * decay + b * weight for a, b in zip(old[1:], found[1:]))


def late_kernel(count, places, parts, offs_hbm, query, *refs):
    state_in, arrays, refs = refs[:3], refs[3 : 3 + count], refs[3 + count :]
    before, outs, (offs, *state, ratio, chosen, sems) = refs[:parts], refs[parts : 2 * parts], refs[2 * parts :]
    heads, n3 = state[0].shape[:2]
    n4 = n3 // 2
    me = lax.axis_index("head")
    offs_load = Copies(sems).start(offs_hbm, offs)
    third, fourth = LATE
    found = []
    for head in range(heads):
        spans = (slice(0, n3), slice(n3, n3 + n4))
        for places_of, span in zip(places, spans):
            keys, values = branch_of(arrays, places_of, head)
            found.append(attend(query[head, span, :], keys, values))
    for head in range(heads):
        new = joined_state([ref[head, :n3, :] for ref in state_in], found[2 * head])
        for ref, array in zip(state, new):
            ref[head] = array
        ratio[head, :n3, :] = new[2] / new[1]
    offs_load.wait()
    for head in range(heads):
        offset = offs[fourth, me * heads + head]
        nested = (offset & ((1 << third) - 1)) == offs[third, me * heads + head]
        inner = pl.ds(offset >> third, n4, stride=2)
        old = [
            jnp.where(nested, ref[head, inner, :], given[head, n3:, :])
            for ref, given in zip(state, state_in)
        ]
        new = joined_state(old, found[2 * head + 1])
        ratio[head, n3:, :] = new[2] / new[1]
        for d in range(parts):
            low = 0
            for start, n in ((0, n3 // parts), (n3, n4 // parts)):
                chosen[low : low + n, :] = ratio[head, pl.ds(start + (me ^ d) * n, n), :]
                low += n
            known = before[d].shape[1]
            outs[d][head, :known] = before[d][head]
            outs[d][head, known:] = chosen[...].astype(BF16)


def late(offsets, rows, query, state, pieces, before):
    heads = query.shape[0]
    arrays, places = operands(pieces)
    parts = len(before)
    chosen = compact_rows(LATE, rows // parts)
    n3 = rows >> LATE[0]
    return pl.pallas_call(
        functools.partial(late_kernel, len(arrays), places, parts),
        in_specs=[HBM] + [VMEM] * (4 + len(arrays) + parts),
        out_specs=[VMEM] * parts,
        out_shape=[shape(heads, compact_rows(LATER, rows // parts), HD)] * parts,
        scratch_shapes=[
            pltpu.SMEM(offsets.shape, jnp.int32),
            pltpu.VMEM((heads, n3, HD), F32),
            pltpu.VMEM((heads, n3, HD), F32),
            pltpu.VMEM((heads, n3, HD), F32),
            pltpu.VMEM((heads, compact_rows(LATE, rows), HD), F32),
            pltpu.VMEM((chosen, HD), F32),
            pltpu.SemaphoreType.DMA((1,)),
        ],
        compiler_params=pltpu.CompilerParams(vmem_limit_bytes=VMEM_LIMIT),
        cost_estimate=cost(0.01),
        name="late",
    )(in_hbm(offsets), query, *state, *arrays, *before)


def mix_kernel(distances, heads, split, last, offs_in, *refs):
    count = len(distances)
    early_refs, later_refs, refs = refs[:count], refs[count : 2 * count], refs[2 * count :]
    total = None
    if refs[0].dtype == F32:
        total, refs = refs[0], refs[1:]
    w_refs, (out, offs, wide, narrow, joined, ready, sems) = refs[:-7], refs[-7:]
    rows = out.shape[0]
    me = lax.axis_index("head")
    copies = Copies(sems)
    offs_load = copies.start(offs_in, offs)
    for i, d in enumerate(distances):
        for head in range(heads):
            wide[head] = early_refs[i][:, head * HD : (head + 1) * HD].astype(F32)
            narrow[head] = later_refs[i][head].astype(F32)
        if i == 0:
            offs_load.wait()
        for head in range(heads):
            low = 0
            for b in LATER:
                picked = pick(offs, b, (me ^ d) * heads + head, rows)
                wide[head, picked, :] = narrow[head, low : low + picked.size, :]
                low += picked.size
            joined[i, :, head * HD : (head + 1) * HD] = wide[head].astype(BF16)
    weights = [ref[...] for ref in w_refs]
    if split:
        part = lax.rem(lax.axis_index("seq"), 2)
        depth = weights[0].shape[0]
        columns = [pl.ds(pl.multiple_of((part ^ c) * depth, depth), depth) for c in range(2)]
        weights = [jnp.concatenate(weights, axis=0)]
    step = rows // CHUNKS if rows % (16 * CHUNKS) == 0 else rows
    stores = []
    for low in range(0, rows, step):
        span = pl.ds(low, step)
        found = None if total is None else total[span, :]
        for i, weight in enumerate(weights):
            left = joined[i, span, :]
            if split:
                left = jnp.concatenate([joined[i, span, c] for c in columns], axis=1)
            term = jnp.dot(left, weight, preferred_element_type=F32)
            found = term if found is None else found + term
        if last:
            ready[span, :] = found.astype(out.dtype)
            stores.append(copies.start(ready.at[span], out.at[span]))
        else:
            out[span, :] = found.astype(out.dtype)
    wait_all(stores)


def mix(offsets, distances, early_parts, later_parts, weights, total, last):
    heads = later_parts[0].shape[0]
    rows, width = early_parts[0].shape[0], weights[0].shape[1]
    split = len(weights) > len(distances)
    totals = [] if total is None else [total]
    arrays = [*early_parts, *later_parts, *totals, *weights]
    return pl.pallas_call(
        functools.partial(mix_kernel, distances, heads, split, last),
        in_specs=[VMEM] * (1 + len(arrays)),
        out_specs=ANY if last else VMEM,
        out_shape=shape(rows, width, dtype=BF16 if last else F32),
        scratch_shapes=[
            pltpu.SMEM(offsets.shape, jnp.int32),
            pltpu.VMEM((heads, rows, HD), F32),
            pltpu.VMEM((heads, compact_rows(LATER, rows), HD), F32),
            pltpu.VMEM((len(distances), rows, heads * HD), BF16),
            pltpu.VMEM((rows, width) if last else (16, HD), BF16),
            pltpu.SemaphoreType.DMA((1 + CHUNKS,)),
        ],
        compiler_params=pltpu.CompilerParams(vmem_limit_bytes=VMEM_LIMIT),
        cost_estimate=cost(1),
        name="mix",
    )(offsets, *arrays)


def swap(x, axis, distance):
    return lax.ppermute(x, axis, [(i, i ^ distance) for i in range(lax.axis_size(axis))])


def together(arrays):
    return list(lax.optimization_barrier(tuple(arrays)))


def pair(piece):
    return [piece, swap(piece, "seq", 1)]


def layer_16(tokens, w_qkv, w_out, offsets):
    parts = lax.axis_size("head")
    rows = tokens.shape[0]
    n1, n2, n3, n4 = (rows >> b for b in range(1, NB))
    groups = [(1, 4, 3, 2), (4, 3, 2), (4, 3), (4,)]
    tokens, near_offsets, kv, near, all_own, far, b4, w_half = project(
        offsets, tokens, w_qkv, w_out, groups, True
    )
    near_core = swap(near, "seq", 1)
    b4_z8, b4_z12 = swap(b4, "seq", 8), swap(b4, "seq", 12)
    far_z4 = swap(far, "seq", 4)
    w_half = swap(w_half, "head", 1)
    all_y = swap(all_own, "seq", 2)
    nears = [near, near_core]
    pieces = [[(kv, 0, rows)], [(piece, 0, n1) for piece in nears]]
    first, other, query, *state = early(offsets, tokens, w_qkv, pieces, parts)
    all_y, far_z4, b4_z8, b4_z12, query = together([all_y, far_z4, b4_z8, b4_z12, query])
    b4_z = jnp.concatenate([b4_z8, b4_z12], axis=1)
    b4_yz = swap(b4_z, "seq", 2)
    far_yz4 = swap(all_y[:, : n4 + n3], "seq", 4)
    alls, far_z4s, b4_zs = pair(all_y), pair(far_z4), pair(b4_z)
    alls[1], far_z4s[1], b4_zs[1] = together([alls[1], far_z4s[1], b4_zs[1]])
    pieces = [
        [(piece, n1 + n4 + n3, n2) for piece in nears] + [(piece, n4 + n3, n2) for piece in alls]
    ]
    *middle_parts, query, top, row_sum, value = middle(
        offsets, rows, query, state, pieces, parts
    )
    state = [top, row_sum, value]
    other = swap(other, "head", 1)
    far_yz4, b4_yz, query = together([far_yz4, b4_yz, query])
    fars = alls + far_z4s + pair(far_yz4)
    b4_zs = b4_zs + pair(b4_yz)
    pieces = [
        [(piece, n1 + n4, n3) for piece in nears] + [(piece, n4, n3) for piece in fars],
        [(piece, n1, n4) for piece in nears]
        + [(piece, 0, n4) for piece in fars]
        + [(piece, 0, 2 * n4) for piece in b4_zs],
    ]
    late_parts = late(offsets, rows, query, state, pieces, middle_parts)
    w_half, other, *late_parts = together([w_half, other, *late_parts])
    late_part = swap(late_parts[1], "head", 1)
    total = mix(near_offsets, [0], [first], late_parts[:1], [w_out], None, False)
    weights = [w_half, swap(w_half, "seq", 1)]
    return mix(near_offsets, [1], [other], [late_part], weights, total, True)


def exchange(own, seq):
    gathered = []
    for b in range(NB):
        pieces = own[b]
        for step in range((seq * (1 << b) // 16).bit_length() - 1):
            pieces = jnp.concatenate([pieces, swap(pieces, "seq", 1 << step)], axis=1)
        gathered.append([(pieces, 0, pieces.shape[1])])
    return gathered


def on_device(tokens, w_qkv, w_out, offsets):
    seq, parts = lax.axis_size("seq"), lax.axis_size("head")
    rows = tokens.shape[0]
    if seq == 16 and parts == 2:
        return layer_16(tokens, w_qkv, w_out, offsets)
    groups = [(b,) for b in range(1, NB)]
    tokens, near_offsets, *own = project(offsets, tokens, w_qkv, w_out, groups, False)
    gathered = exchange(own, seq)
    weights = [w_out] + [swap(w_out, "head", d) for d in range(1, parts)]
    *early_parts, query, top, row_sum, value = early(
        offsets, tokens, w_qkv, gathered[:2], parts
    )
    state = [top, row_sum, value]
    *middle_parts, query, top, row_sum, value = middle(
        offsets, rows, query, state, gathered[2:3], parts
    )
    state = [top, row_sum, value]
    late_parts = list(late(offsets, rows, query, state, gathered[3:], middle_parts))
    for found in (early_parts, late_parts):
        found[1:] = [swap(found[d], "head", d) for d in range(1, parts)]
    return mix(near_offsets, list(range(parts)), early_parts, late_parts, weights, None, True)


def solution(mesh):
    in_specs = (P("seq", None), P(None, "head"), P("head", None), P())
    out_specs = P(("seq", "head"), None)
    return jax.shard_map(
        on_device, mesh=mesh, in_specs=in_specs, out_specs=out_specs, check_vma=False
    )
```

```python
import functools
import math

import jax
import jax.numpy as jnp
from jax import lax
from jax.experimental import pallas as pl
from jax.experimental.pallas import tpu as pltpu
from jax.sharding import PartitionSpec as P

HD = 128
NB = 5
MIDDLE, LATE = (2,), (3, 4)
LATER = MIDDLE + LATE
BF16 = jnp.bfloat16
F32 = jnp.float32
UNIT = math.log2(math.e) / math.sqrt(HD)
VMEM_LIMIT = 24 << 20
CHUNKS = 2
ANY = pl.BlockSpec(memory_space=pl.ANY)
VMEM = pl.BlockSpec(memory_space=pltpu.VMEM)
HBM = pl.BlockSpec(memory_space=pltpu.HBM)


def shape(*extent, dtype=BF16):
    return jax.ShapeDtypeStruct(extent, dtype)


class Copies:
    def __init__(self, sems):
        self.sems = sems
        self.used = 0

    def start(self, source, target):
        copy = pltpu.make_async_copy(source, target, self.sems.at[self.used])
        self.used += 1
        copy.start()
        return copy


def wait_all(copies):
    for copy in copies:
        copy.wait()


def in_hbm(x):
    return pltpu.with_memory_space_constraint(x, pltpu.HBM)


def cost(microseconds):
    return pl.CostEstimate(
        flops=int(microseconds * 1e9), bytes_accessed=0, transcendentals=0
    )


def project_kernel(groups, halves, offs_hbm, tok_hbm, w_hbm, wo_hbm, *refs):
    heads = w_hbm.shape[1] // (3 * HD)
    rows = tok_hbm.shape[0]
    outs, (offs, w, wide, sems) = refs[:-4], refs[-4:]
    tok, offs_out, outs = outs[0], outs[1], outs[2:]
    first = lax.axis_index("head") * heads
    copies = Copies(sems)
    step = min(heads, 2)
    half = tok.shape[1] // 2
    tok_loads, loads = [], []
    for low in (0, half):
        depth = pl.ds(low, half)
        tok_loads.append(copies.start(tok_hbm.at[:, depth], tok.at[:, depth]))
        for head in range(step):
            source = w_hbm.at[depth, pl.ds(head * 3 * HD + HD, 2 * HD)]
            loads.append(copies.start(source, w.at[depth, pl.ds(head * 2 * HD, 2 * HD)]))
    for head in range(step, heads):
        columns = pl.ds(head * 3 * HD + HD, 2 * HD)
        loads.append(copies.start(w_hbm.at[:, columns], w.at[:, pl.ds(head * 2 * HD, 2 * HD)]))
    offs_load = copies.start(offs_hbm, offs)
    stores = [copies.start(offs_hbm, offs_out)]
    if halves:
        depth = wo_hbm.shape[0] // 2
        part = lax.rem(lax.axis_index("seq"), 2)
        source = wo_hbm.at[pl.ds(pl.multiple_of(part * depth, depth), depth)]
        stores.append(copies.start(source, outs[-1]))
    for head in range(heads + step):
        if head < heads and head % step == 0:
            columns = slice(head * 2 * HD, (head + step) * 2 * HD)
            if head == 0:
                both = None
                for i, low in enumerate((0, half)):
                    tok_loads[i].wait()
                    wait_all(loads[i * step : (i + 1) * step])
                    term = jnp.dot(
                        tok[:, low : low + half],
                        w[low : low + half, columns],
                        preferred_element_type=F32,
                    )
                    both = term if both is None else both + term
            else:
                wait_all(loads[head + step : head + 2 * step])
                both = jnp.dot(tok[...], w[:, columns], preferred_element_type=F32)
            both = both.astype(BF16)
            for i in range(2 * step):
                part = both[:, i * HD : (i + 1) * HD]
                outs[0][head + i // 2, :, i % 2 * HD : (i % 2 + 1) * HD] = part
                wide[2 * head + i] = part.astype(F32)
        if head == 0:
            offs_load.wait()
        if head < step:
            continue
        done = head - step
        for b in range(1, NB):
            n = rows >> b
            offset = offs[b, first + done]
            for c in range(2):
                picked = wide[2 * done + c, pl.ds(offset, n, stride=1 << b), :].astype(BF16)
                for out, group in zip(outs[1:], groups):
                    if b in group:
                        low = sum(rows >> other for other in group[: group.index(b)])
                        out[done, low : low + n, c * HD : (c + 1) * HD] = picked
    wait_all(stores)


def project(offsets, tokens, w_qkv, w_out, groups, halves):
    heads = w_qkv.shape[1] // (3 * HD)
    rows, width = tokens.shape
    out_shape = [shape(rows, width), shape(*offsets.shape, dtype=jnp.int32)]
    out_shape.append(shape(heads, rows, 2 * HD))
    for group in groups:
        out_shape.append(shape(heads, sum(rows >> b for b in group), 2 * HD))
    out_specs = [VMEM] * len(out_shape)
    if halves:
        out_shape.append(shape(w_out.shape[0] // 2, w_out.shape[1]))
        out_specs.append(ANY)
    return pl.pallas_call(
        functools.partial(project_kernel, groups, halves),
        in_specs=[HBM, HBM, HBM, HBM],
        out_specs=out_specs,
        out_shape=out_shape,
        scratch_shapes=[
            pltpu.SMEM(offsets.shape, jnp.int32),
            pltpu.VMEM((width, heads * 2 * HD), BF16),
            pltpu.VMEM((2 * heads, rows, HD), F32),
            pltpu.SemaphoreType.DMA((7 + heads,)),
        ],
        compiler_params=pltpu.CompilerParams(vmem_limit_bytes=VMEM_LIMIT),
        cost_estimate=cost(5),
        name="project",
    )(in_hbm(offsets), in_hbm(tokens), in_hbm(w_qkv), in_hbm(w_out))


def keys_and_values(refs, spans, head):
    parts = [ref[head, low : low + n, :] for ref, (low, n) in zip(refs, spans)]
    both = jnp.concatenate(parts, axis=0) if len(parts) > 1 else parts[0]
    ones = jnp.ones((both.shape[0], HD), BF16)
    return both[:, :HD], jnp.concatenate([both[:, HD:], ones], axis=1)


def operands(pieces):
    arrays, places = [], []
    for branch in pieces:
        found = []
        for array, low, n in branch:
            known = [i for i, other in enumerate(arrays) if other is array]
            if not known:
                known = [len(arrays)]
                arrays.append(array)
            found.append((known[0], low, n))
        places.append(found)
    return arrays, places


def branch_of(refs, places, head):
    return keys_and_values([refs[i] for i, _, _ in places], [(low, n) for _, low, n in places], head)


def attend(query, keys, values):
    scores = lax.dot_general(
        query, keys, (((1,), (1,)), ((), ())), preferred_element_type=F32
    )
    top = jnp.max(scores, axis=1, keepdims=True)
    probs = jnp.exp2((scores - top) * UNIT).astype(BF16)
    both = jnp.dot(probs, values, preferred_element_type=F32)
    top = jnp.broadcast_to(top * UNIT, (query.shape[0], HD))
    return top, both[:, HD:], both[:, :HD]


def merge(state, head, picked, found):
    top_ref, sum_ref, value_ref = state
    top, row_sum, value = found
    old = top_ref[head, picked, :]
    new = jnp.maximum(old, top)
    decay, weight = jnp.exp2(old - new), jnp.exp2(top - new)
    top_ref[head, picked, :] = new
    sum_ref[head, picked, :] = sum_ref[head, picked, :] * decay + row_sum * weight
    value_ref[head, picked, :] = value_ref[head, picked, :] * decay + value * weight


def compact_rows(branches, rows):
    return sum(rows >> b for b in branches)


def compact(state, head, picks, outs):
    low = 0
    for picked in picks:
        for ref, out in zip(state, outs):
            out[head, low : low + picked.size, :] = ref[head, picked, :]
        low += picked.size


def pick(offs, b, head, rows):
    return pl.ds(offs[b, head], rows >> b, stride=1 << b)


def early_kernel(count, places, parts, offs_hbm, tok, w_hbm, *refs):
    arrays, refs = refs[:count], refs[count:]
    outs, later_query, later = refs[:parts], refs[parts], refs[parts + 1 : parts + 4]
    offs, w_query, query, *state, sems = refs[parts + 4 :]
    heads, rows = query.shape[:2]
    part_rows = rows // parts
    me = lax.axis_index("head")
    copies = Copies(sems)
    loads = []
    for head in range(heads):
        source = w_hbm.at[:, pl.ds(head * 3 * HD, HD)]
        loads.append(copies.start(source, w_query.at[:, pl.ds(head * HD, HD)]))
    offs_load = copies.start(offs_hbm, offs)
    wait_all(loads)
    projected = jnp.dot(tok[...], w_query[...], preferred_element_type=F32).astype(BF16)
    step = min(rows, 256)
    offs_load.wait()
    for head in range(heads):
        mine = projected[:, head * HD : (head + 1) * HD]
        query[head] = mine.astype(F32)
        keys, values = branch_of(arrays, places[0], head)
        for low in range(0, rows, step):
            span = slice(low, low + step)
            for ref, array in zip(state, attend(mine[span], keys, values)):
                ref[head, span] = array
        keys, values = branch_of(arrays, places[1], head)
        picked = pick(offs, 1, me * heads + head, rows)
        merge(state, head, picked, attend(query[head, picked, :].astype(BF16), keys, values))
        _, row_sum, value = state
        columns = slice(head * HD, (head + 1) * HD)
        for d in range(parts):
            span = pl.ds(pl.multiple_of((me ^ d) * part_rows, part_rows), part_rows)
            outs[d][:, columns] = (value[head, span, :] / row_sum[head, span, :]).astype(BF16)
        picks = [pick(offs, b, me * heads + head, rows) for b in LATER]
        low = 0
        for picked in picks:
            later_query[head, low : low + picked.size, :] = query[head, picked, :].astype(BF16)
            low += picked.size
        compact(state, head, picks, later)


def early(offsets, tokens, w_qkv, pieces, parts):
    heads = w_qkv.shape[1] // (3 * HD)
    rows, width = tokens.shape
    arrays, places = operands(pieces)
    later = compact_rows(LATER, rows)
    out_shape = [shape(rows // parts, heads * HD)] * parts
    out_shape.append(shape(heads, later, HD))
    out_shape += [shape(heads, later, HD, dtype=F32)] * 3
    return pl.pallas_call(
        functools.partial(early_kernel, len(arrays), places, parts),
        in_specs=[HBM, VMEM, HBM] + [VMEM] * len(arrays),
        out_specs=[VMEM] * len(out_shape),
        out_shape=out_shape,
        scratch_shapes=[
            pltpu.SMEM(offsets.shape, jnp.int32),
            pltpu.VMEM((width, heads * HD), BF16),
            pltpu.VMEM((heads, rows, HD), F32),
            pltpu.VMEM((heads, rows, HD), F32),
            pltpu.VMEM((heads, rows, HD), F32),
            pltpu.VMEM((heads, rows, HD), F32),
            pltpu.SemaphoreType.DMA((1 + heads,)),
        ],
        compiler_params=pltpu.CompilerParams(vmem_limit_bytes=VMEM_LIMIT),
        cost_estimate=cost(4),
        name="early",
    )(in_hbm(offsets), tokens, in_hbm(w_qkv), *arrays)


def middle_kernel(count, places, parts, offs_hbm, query, top_in, sum_in, value_in, *refs):
    arrays, refs = refs[:count], refs[count:]
    outs, late_query, late = refs[:parts], refs[parts], refs[parts + 1 : parts + 4]
    offs, *state, sems = refs[parts + 4 :]
    _, row_sum, value = state
    heads, rows = value.shape[:2]
    part_rows = rows // parts
    me = lax.axis_index("head")
    offs_load = Copies(sems).start(offs_hbm, offs)
    (branch,) = MIDDLE
    own = rows >> branch
    found = []
    for head in range(heads):
        keys, values = branch_of(arrays, places[0], head)
        found.append(attend(query[head, :own, :], keys, values))
    offs_load.wait()
    for head in range(heads):
        picks = [pick(offs, b, me * heads + head, rows) for b in LATER]
        low = 0
        for picked in picks:
            for ref, array in zip(state, (top_in, sum_in, value_in)):
                ref[head, picked, :] = array[head, low : low + picked.size, :]
            low += picked.size
        merge(state, head, picks[0], found[head])
        for d in range(parts):
            start = (me ^ d) * part_rows + offs[branch, me * heads + head]
            source = pl.ds(start, part_rows >> branch, stride=1 << branch)
            outs[d][head] = (value[head, source, :] / row_sum[head, source, :]).astype(BF16)
        late_query[head] = query[head, own:, :]
        compact(state, head, picks[1:], late)


def middle(offsets, rows, query, state, pieces, parts):
    heads = query.shape[0]
    arrays, places = operands(pieces)
    late = compact_rows(LATE, rows)
    out_shape = [shape(heads, compact_rows(MIDDLE, rows // parts), HD)] * parts
    out_shape.append(shape(heads, late, HD))
    out_shape += [shape(heads, late, HD, dtype=F32)] * 3
    return pl.pallas_call(
        functools.partial(middle_kernel, len(arrays), places, parts),
        in_specs=[HBM] + [VMEM] * (4 + len(arrays)),
        out_specs=[VMEM] * len(out_shape),
        out_shape=out_shape,
        scratch_shapes=[
            pltpu.SMEM(offsets.shape, jnp.int32),
            pltpu.VMEM((heads, rows, HD), F32),
            pltpu.VMEM((heads, rows, HD), F32),
            pltpu.VMEM((heads, rows, HD), F32),
            pltpu.SemaphoreType.DMA((1,)),
        ],
        compiler_params=pltpu.CompilerParams(vmem_limit_bytes=VMEM_LIMIT),
        cost_estimate=cost(0.01),
        name="middle",
    )(in_hbm(offsets), query, *state, *arrays)


def joined_state(old, found):
    top = jnp.maximum(old[0], found[0])
    decay, weight = jnp.exp2(old[0] - top), jnp.exp2(found[0] - top)
    return top, *(a * decay + b * weight for a, b in zip(old[1:], found[1:]))


def late_kernel(count, places, parts, offs_hbm, query, *refs):
    state_in, arrays, refs = refs[:3], refs[3 : 3 + count], refs[3 + count :]
    before, outs, (offs, *state, ratio, chosen, sems) = refs[:parts], refs[parts : 2 * parts], refs[2 * parts :]
    heads, n3 = state[0].shape[:2]
    n4 = n3 // 2
    me = lax.axis_index("head")
    offs_load = Copies(sems).start(offs_hbm, offs)
    third, fourth = LATE
    found = []
    for head in range(heads):
        spans = (slice(0, n3), slice(n3, n3 + n4))
        for places_of, span in zip(places, spans):
            keys, values = branch_of(arrays, places_of, head)
            found.append(attend(query[head, span, :], keys, values))
    for head in range(heads):
        new = joined_state([ref[head, :n3, :] for ref in state_in], found[2 * head])
        for ref, array in zip(state, new):
            ref[head] = array
        ratio[head, :n3, :] = new[2] / new[1]
    offs_load.wait()
    for head in range(heads):
        offset = offs[fourth, me * heads + head]
        nested = (offset & ((1 << third) - 1)) == offs[third, me * heads + head]
        inner = pl.ds(offset >> third, n4, stride=2)
        old = [
            jnp.where(nested, ref[head, inner, :], given[head, n3:, :])
            for ref, given in zip(state, state_in)
        ]
        new = joined_state(old, found[2 * head + 1])
        ratio[head, n3:, :] = new[2] / new[1]
        for d in range(parts):
            low = 0
            for start, n in ((0, n3 // parts), (n3, n4 // parts)):
                chosen[low : low + n, :] = ratio[head, pl.ds(start + (me ^ d) * n, n), :]
                low += n
            known = before[d].shape[1]
            outs[d][head, :known] = before[d][head]
            outs[d][head, known:] = chosen[...].astype(BF16)


def late(offsets, rows, query, state, pieces, before):
    heads = query.shape[0]
    arrays, places = operands(pieces)
    parts = len(before)
    chosen = compact_rows(LATE, rows // parts)
    n3 = rows >> LATE[0]
    return pl.pallas_call(
        functools.partial(late_kernel, len(arrays), places, parts),
        in_specs=[HBM] + [VMEM] * (4 + len(arrays) + parts),
        out_specs=[VMEM] * parts,
        out_shape=[shape(heads, compact_rows(LATER, rows // parts), HD)] * parts,
        scratch_shapes=[
            pltpu.SMEM(offsets.shape, jnp.int32),
            pltpu.VMEM((heads, n3, HD), F32),
            pltpu.VMEM((heads, n3, HD), F32),
            pltpu.VMEM((heads, n3, HD), F32),
            pltpu.VMEM((heads, compact_rows(LATE, rows), HD), F32),
            pltpu.VMEM((chosen, HD), F32),
            pltpu.SemaphoreType.DMA((1,)),
        ],
        compiler_params=pltpu.CompilerParams(vmem_limit_bytes=VMEM_LIMIT),
        cost_estimate=cost(0.01),
        name="late",
    )(in_hbm(offsets), query, *state, *arrays, *before)


def mix_kernel(distances, heads, split, last, offs_in, *refs):
    count = len(distances)
    early_refs, later_refs, refs = refs[:count], refs[count : 2 * count], refs[2 * count :]
    total = None
    if refs[0].dtype == F32:
        total, refs = refs[0], refs[1:]
    w_refs, (out, offs, wide, narrow, joined, ready, sems) = refs[:-7], refs[-7:]
    rows = out.shape[0]
    me = lax.axis_index("head")
    copies = Copies(sems)
    offs_load = copies.start(offs_in, offs)
    for i, d in enumerate(distances):
        for head in range(heads):
            wide[head] = early_refs[i][:, head * HD : (head + 1) * HD].astype(F32)
            narrow[head] = later_refs[i][head].astype(F32)
        if i == 0:
            offs_load.wait()
        for head in range(heads):
            low = 0
            for b in LATER:
                picked = pick(offs, b, (me ^ d) * heads + head, rows)
                wide[head, picked, :] = narrow[head, low : low + picked.size, :]
                low += picked.size
            joined[i, :, head * HD : (head + 1) * HD] = wide[head].astype(BF16)
    weights = [ref[...] for ref in w_refs]
    if split:
        part = lax.rem(lax.axis_index("seq"), 2)
        depth = weights[0].shape[0]
        columns = [pl.ds(pl.multiple_of((part ^ c) * depth, depth), depth) for c in range(2)]
        weights = [jnp.concatenate(weights, axis=0)]
    step = rows // CHUNKS if rows % (16 * CHUNKS) == 0 else rows
    stores = []
    for low in range(0, rows, step):
        span = pl.ds(low, step)
        found = None if total is None else total[span, :]
        for i, weight in enumerate(weights):
            left = joined[i, span, :]
            if split:
                left = jnp.concatenate([joined[i, span, c] for c in columns], axis=1)
            term = jnp.dot(left, weight, preferred_element_type=F32)
            found = term if found is None else found + term
        if last:
            ready[span, :] = found.astype(out.dtype)
            stores.append(copies.start(ready.at[span], out.at[span]))
        else:
            out[span, :] = found.astype(out.dtype)
    wait_all(stores)


def mix(offsets, distances, early_parts, later_parts, weights, total, last):
    heads = later_parts[0].shape[0]
    rows, width = early_parts[0].shape[0], weights[0].shape[1]
    split = len(weights) > len(distances)
    totals = [] if total is None else [total]
    arrays = [*early_parts, *later_parts, *totals, *weights]
    return pl.pallas_call(
        functools.partial(mix_kernel, distances, heads, split, last),
        in_specs=[VMEM] * (1 + len(arrays)),
        out_specs=ANY if last else VMEM,
        out_shape=shape(rows, width, dtype=BF16 if last else F32),
        scratch_shapes=[
            pltpu.SMEM(offsets.shape, jnp.int32),
            pltpu.VMEM((heads, rows, HD), F32),
            pltpu.VMEM((heads, compact_rows(LATER, rows), HD), F32),
            pltpu.VMEM((len(distances), rows, heads * HD), BF16),
            pltpu.VMEM((rows, width) if last else (16, HD), BF16),
            pltpu.SemaphoreType.DMA((1 + CHUNKS,)),
        ],
        compiler_params=pltpu.CompilerParams(vmem_limit_bytes=VMEM_LIMIT),
        cost_estimate=cost(1),
        name="mix",
    )(offsets, *arrays)


def swap(x, axis, distance):
    return lax.ppermute(x, axis, [(i, i ^ distance) for i in range(lax.axis_size(axis))])


def together(arrays):
    return list(lax.optimization_barrier(tuple(arrays)))


def pair(piece):
    return [piece, swap(piece, "seq", 1)]


def layer_16(tokens, w_qkv, w_out, offsets):
    parts = lax.axis_size("head")
    rows = tokens.shape[0]
    n1, n2, n3, n4 = (rows >> b for b in range(1, NB))
    groups = [(1, 4, 3, 2), (4, 3, 2), (4, 3), (4,)]
    tokens, near_offsets, kv, near, all_own, far, b4, w_half = project(
        offsets, tokens, w_qkv, w_out, groups, True
    )
    near_core = swap(near, "seq", 1)
    b4_z8, b4_z12 = swap(b4, "seq", 8), swap(b4, "seq", 12)
    far_z4 = swap(far, "seq", 4)
    w_half = swap(w_half, "head", 1)
    all_y = swap(all_own, "seq", 2)
    nears = [near, near_core]
    pieces = [[(kv, 0, rows)], [(piece, 0, n1) for piece in nears]]
    first, other, query, *state = early(offsets, tokens, w_qkv, pieces, parts)
    all_y, far_z4, b4_z8, b4_z12, query = together([all_y, far_z4, b4_z8, b4_z12, query])
    b4_z = jnp.concatenate([b4_z8, b4_z12], axis=1)
    b4_yz = swap(b4_z, "seq", 2)
    far_yz4 = swap(all_y[:, : n4 + n3], "seq", 4)
    alls, far_z4s, b4_zs = pair(all_y), pair(far_z4), pair(b4_z)
    alls[1], far_z4s[1], b4_zs[1] = together([alls[1], far_z4s[1], b4_zs[1]])
    pieces = [
        [(piece, n1 + n4 + n3, n2) for piece in nears] + [(piece, n4 + n3, n2) for piece in alls]
    ]
    *middle_parts, query, top, row_sum, value = middle(
        offsets, rows, query, state, pieces, parts
    )
    state = [top, row_sum, value]
    other = swap(other, "head", 1)
    far_yz4, b4_yz, query = together([far_yz4, b4_yz, query])
    fars = alls + far_z4s + pair(far_yz4)
    b4_zs = b4_zs + pair(b4_yz)
    pieces = [
        [(piece, n1 + n4, n3) for piece in nears] + [(piece, n4, n3) for piece in fars],
        [(piece, n1, n4) for piece in nears]
        + [(piece, 0, n4) for piece in fars]
        + [(piece, 0, 2 * n4) for piece in b4_zs],
    ]
    late_parts = late(offsets, rows, query, state, pieces, middle_parts)
    w_half, other, *late_parts = together([w_half, other, *late_parts])
    late_part = swap(late_parts[1], "head", 1)
    total = mix(near_offsets, [0], [first], late_parts[:1], [w_out], None, False)
    weights = [w_half, swap(w_half, "seq", 1)]
    return mix(near_offsets, [1], [other], [late_part], weights, total, True)


def exchange(own, seq):
    gathered = []
    for b in range(NB):
        pieces = own[b]
        for step in range((seq * (1 << b) // 16).bit_length() - 1):
            pieces = jnp.concatenate([pieces, swap(pieces, "seq", 1 << step)], axis=1)
        gathered.append([(pieces, 0, pieces.shape[1])])
    return gathered


def on_device(tokens, w_qkv, w_out, offsets):
    seq, parts = lax.axis_size("seq"), lax.axis_size("head")
    rows = tokens.shape[0]
    if seq == 16 and parts == 2:
        return layer_16(tokens, w_qkv, w_out, offsets)
    groups = [(b,) for b in range(1, NB)]
    tokens, near_offsets, *own = project(offsets, tokens, w_qkv, w_out, groups, False)
    gathered = exchange(own, seq)
    weights = [w_out] + [swap(w_out, "head", d) for d in range(1, parts)]
    *early_parts, query, top, row_sum, value = early(
        offsets, tokens, w_qkv, gathered[:2], parts
    )
    state = [top, row_sum, value]
    *middle_parts, query, top, row_sum, value = middle(
        offsets, rows, query, state, gathered[2:3], parts
    )
    state = [top, row_sum, value]
    late_parts = list(late(offsets, rows, query, state, gathered[3:], middle_parts))
    for found in (early_parts, late_parts):
        found[1:] = [swap(found[d], "head", d) for d in range(1, parts)]
    return mix(near_offsets, list(range(parts)), early_parts, late_parts, weights, None, True)


def solution(mesh):
    in_specs = (P("seq", None), P(None, "head"), P("head", None), P())
    out_specs = P(("seq", "head"), None)
    return jax.shard_map(
        on_device, mesh=mesh, in_specs=in_specs, out_specs=out_specs, check_vma=False
    )
```
